128 devices in a mesh: tm: 32 (over z, y, core), space: 4 (over x).
Axes of the slice: x: 4, y: 4, z: 4, core: 2. Of those that a mesh axis runs over, the one named last changes fastest.
Arguments:
- tokens: bfloat16 [65536, 2240], P('tm'), may hold values from -6 to 6
- mod_scale: float32 [2240], replicated, may hold values from -1.5 to 1.5
- mod_shift: float32 [2240], replicated, may hold values from -3 to 3
- out_gate: float32 [2240], replicated, may hold values from -4 to 4
- w_query: bfloat16 [2240, 2240], P(None, 'space'), may hold values from -0.125 to 0.125
- w_key: bfloat16 [2240, 2240], P(None, 'space'), may hold values from -0.125 to 0.125
- w_value: bfloat16 [2240, 2240], P(None, 'space'), may hold values from -0.125 to 0.125
- w_out: bfloat16 [2240, 2240], P('space'), may hold values from -0.125 to 0.125
- log_decay: float32 [128, 20], P('tm', 'space'), may hold values from -8 to 0
- mix_weight: bfloat16 [8, 16, 16], replicated, may hold values from -0.5 to 0.5
- block_last: int32 [128], P('tm'), may hold values from 0 to 127, as said below
- win_list: int32 [128, 32, 8], replicated, may hold values from 0 to 127, as said below
Outputs:
- out: bfloat16 [65536, 2240], P(('tm', 'space'))
The draws below stay inside these ranges and needn't reach their ends.
Inputs may be any that keep to these rules, and one draw needn't show every extreme that they name: `block_last`: frame blocks are runs of consecutive frames that never cross a boundary between the groups of 4 frames that start at multiples of 4; each entry is at least its own frame's index and at most the last frame of that group. `win_list`: every listed frame lies within 2 frames of the frame that lists it; slot 0 names the frame 2 earlier and slot 1 the frame 2 later, each clipped to 0 .. 127.
All inputs are finite; a program needn't handle non-finite values.
Results may differ from the reference program's by a relative error of at most 0.015.
Values may be sent and summed in bfloat16 or wider, within the bound.
A program may use at most 192 MiB of HBM per device.

```python
import jax
import jax.numpy as jnp
from jax import lax

D = 2240
HEAD_COUNT = 20
HEAD_DIM = 112
FD = 4
TILES = 32
TT = 16
NBR = 8
WIN = 2
FRAME_TOTAL = 128
TOKENS = 65536
N_SPACE = 4


def draw_tokens(key, part):
    key = jax.random.fold_in(key, 11)
    jitter_key, offset_key = jax.random.split(key, 2)
    row_frame = jnp.arange(TOKENS, dtype=jnp.int32) // (TILES * TT)
    segment = row_frame * 4 // FRAME_TOTAL
    offsets = 0.5 * jax.random.normal(offset_key, (4, D), jnp.float32)
    shifted = jnp.take(offsets, segment, axis=0)
    jitter = jax.random.normal(jitter_key, (TOKENS, D), jnp.float32)
    return jnp.clip(jitter + shifted, -6.0, 6.0).astype(jnp.bfloat16)


def draw_block_last(key, part):
    key = jax.random.fold_in(key, 3)
    frame_index = jnp.arange(FRAME_TOTAL, dtype=jnp.int32)
    coins = jax.random.randint(key, (FRAME_TOTAL,), 0, 2, dtype=jnp.int32)
    closes = (coins == 1) | (frame_index % FD == FD - 1)
    marks = jnp.where(closes, frame_index, FRAME_TOTAL - 1)
    return lax.cummin(marks, axis=0, reverse=True).astype(jnp.int32)


def draw_win_list(key, part):
    key = jax.random.fold_in(key, 5)
    offsets = jax.random.randint(key, (FRAME_TOTAL, TILES, NBR), -WIN, WIN + 1, dtype=jnp.int32)
    slot_index = jnp.arange(NBR, dtype=jnp.int32)[None, None, :]
    offsets = jnp.where(slot_index == 0, -WIN, jnp.where(slot_index == 1, WIN, offsets))
    frame_index = jnp.arange(FRAME_TOTAL, dtype=jnp.int32)[:, None, None]
    return jnp.clip(frame_index + offsets, 0, FRAME_TOTAL - 1).astype(jnp.int32)


def draw_log_decay(key, part):
    key = jax.random.fold_in(key, 7)
    selection_random_key, gradual_random_key, quick_random_key, grouping_random_key, jagged_random_key, spike_random_key, penalty_random_key = jax.random.split(key, 7)
    chooser = jax.random.uniform(selection_random_key, (HEAD_COUNT,))
    fast_share = 0.4
    slow_rate = jnp.exp(jax.random.uniform(gradual_random_key, (HEAD_COUNT,), minval=-2.3, maxval=-1.2)) * (2.302585 / FRAME_TOTAL)
    fast_rate = jnp.exp(jax.random.uniform(quick_random_key, (HEAD_COUNT,), minval=-0.69, maxval=0.4))
    per_head_decay = jnp.where(chooser < fast_share, fast_rate, slow_rate)
    grouping_ratio = jnp.exp(jax.random.uniform(grouping_random_key, (FRAME_TOTAL // FD, HEAD_COUNT), minval=-0.7, maxval=0.7))
    grouping_ratio = jnp.repeat(grouping_ratio, FD, axis=0)
    jaggedness = jnp.exp(jax.random.uniform(jagged_random_key, (FRAME_TOTAL, HEAD_COUNT), minval=-0.35, maxval=0.35))
    spike_events = jax.random.uniform(spike_random_key, (FRAME_TOTAL, 1)) < 3.0 / FRAME_TOTAL
    spike_penalty = jnp.log(jax.random.uniform(penalty_random_key, (FRAME_TOTAL, HEAD_COUNT), minval=0.5, maxval=0.8))
    return (-per_head_decay[None, :] * grouping_ratio * jaggedness + jnp.where(spike_events, spike_penalty, 0.0)).astype(jnp.float32)


def shard_levels(stream_key, shape, cuts, least, high):
    def one(position, parts):
        heights = jax.random.uniform(jax.random.fold_in(jax.random.fold_in(stream_key, 6), position), (parts,), jnp.float32, least / len(cuts), high / len(cuts))
        return jnp.repeat(jnp.exp(heights), shape[position] // parts).reshape((-1,) + (1,) * (len(shape) - position - 1))

    loudness = one(*cuts[0])
    for cut in cuts[1:]:
        loudness = loudness * one(*cut)
    return loudness


def centred(rng, extent, spread, bound, cuts=(), kind=jnp.bfloat16):
    array = jax.random.normal(rng, extent, jnp.float32) * spread
    if len(cuts) > 0:
        array = shard_levels(rng, extent, cuts, -0.22, 0.18) * array
    return jnp.clip(array, min=-bound, max=bound).astype(kind)


def setup_inputs(seed: int = 0) -> dict:
    key_list = jax.random.split(jax.random.key(seed), 13)
    tokens = draw_tokens(jax.random.fold_in(key_list[12], 71), 0)
    mod_scale = centred(key_list[1], (D,), 0.3, 1.5, (), jnp.float32)
    mod_shift = centred(key_list[2], (D,), 0.5, 3.0, (), jnp.float32)
    out_gate = centred(key_list[3], (D,), 1.0, 4.0, (), jnp.float32)
    w_query = centred(key_list[4], (D, D), D ** -0.5, 0.125, ((1, 4),))
    w_key = centred(key_list[5], (D, D), D ** -0.5, 0.125, ((1, 4),))
    w_value = centred(key_list[6], (D, D), D ** -0.5, 0.125, ((1, 4),))
    w_out = centred(key_list[7], (D, D), D ** -0.5, 0.125, ((0, 4),))
    log_decay = draw_log_decay(jax.random.fold_in(key_list[12], 71), 0)
    mix_weight = centred(key_list[9], (NBR, TT, TT), (NBR * TT) ** -0.5, 0.5)
    block_last = draw_block_last(jax.random.fold_in(key_list[12], 71), 0)
    win_list = draw_win_list(jax.random.fold_in(key_list[12], 71), 0)
    return dict(tokens=tokens, mod_scale=mod_scale, mod_shift=mod_shift, out_gate=out_gate, w_query=w_query, w_key=w_key, w_value=w_value, w_out=w_out, log_decay=log_decay, mix_weight=mix_weight, block_last=block_last, win_list=win_list)


epsilon = 1e-06
highest = lax.Precision.HIGHEST

def unit_rms(values):
    return values * lax.rsqrt(lax.optimization_barrier(jnp.mean(values * values, axis=-1, keepdims=True)) + epsilon)

def frame_outer(pair):
    return jnp.einsum('thd,the->hde', pair[0].astype(jnp.float32), pair[1].astype(jnp.float32), precision=highest)

def frame_read(pair):
    return unit_rms(jnp.einsum('thd,hde->the', pair[0].astype(jnp.float32), pair[1], precision=highest))

def reference(tokens, mod_scale, mod_shift, out_gate, w_query, w_key, w_value, w_out, log_decay, mix_weight, block_last, win_list):
    normed = (unit_rms(tokens.astype(jnp.float32)) * (1.0 + mod_scale) + mod_shift).astype(jnp.bfloat16)
    queries = jnp.dot(normed, w_query, preferred_element_type=jnp.float32).astype(jnp.bfloat16)
    key_proj = jnp.dot(normed, w_key, preferred_element_type=jnp.float32).astype(jnp.bfloat16)
    values = jnp.dot(normed, w_value, preferred_element_type=jnp.float32).astype(jnp.bfloat16)
    head_shape = (FRAME_TOTAL, TILES * TT, HEAD_COUNT, HEAD_DIM)
    kv_frames = lax.map(frame_outer, (key_proj.reshape(head_shape), values.reshape(head_shape)))

    def advance(running_state, inputs):
        decay_log, fresh_kv = inputs
        running_state = jnp.exp(decay_log)[:, None, None] * running_state + fresh_kv
        return (running_state, running_state)
    zero_state = jnp.zeros((HEAD_COUNT, HEAD_DIM, HEAD_DIM), jnp.float32)
    _, states = lax.scan(advance, zero_state, (log_decay, kv_frames))
    read_states = jnp.take(states, block_last.astype(jnp.int32), axis=0)
    linear = lax.map(frame_read, (queries.reshape(head_shape), read_states)).reshape(TOKENS, D)
    value_tiles = values.reshape(FRAME_TOTAL, TILES, TT, D)
    tile_index = jnp.arange(TILES, dtype=jnp.int32)[:, None]
    mix_float = mix_weight.astype(jnp.float32)

    def mix_frame(frame_lists):
        picked = value_tiles[frame_lists.astype(jnp.int32), tile_index].astype(jnp.float32)
        return jnp.einsum('npq,jnqc->jpc', mix_float, picked, precision=highest).astype(jnp.bfloat16)
    window = lax.map(mix_frame, win_list).reshape(TOKENS, D)
    mixed_heads = (linear + window.astype(jnp.float32)).astype(jnp.bfloat16)
    group_width = D // N_SPACE
    summed = jnp.zeros((TOKENS, D), jnp.float32)
    for group_index in range(N_SPACE):
        low = group_index * group_width
        product = jnp.dot(mixed_heads[:, low:low + group_width], w_out[low:low + group_width], preferred_element_type=jnp.float32)
        summed = summed + lax.optimization_barrier(product.astype(jnp.bfloat16)).astype(jnp.float32)
    return (tokens.astype(jnp.float32) + out_gate * summed).astype(jnp.bfloat16)
```

```python
import jax
import jax.numpy as jnp
from jax import lax
from jax.experimental import pallas as pl
from jax.experimental.pallas import tpu as pltpu
from jax.sharding import PartitionSpec as P

HD = 112
HP = 128
NH = 5
GW = NH * HP
D = 2240
DP = 2304
HALF = DP // 2
FR = 4
ROWS = 512
TILES = 32
TT = 16
NBR = 8
WIN = 2
EPS = 1e-06
RELS = (0, 2, 3, 1)
MESH = pl.DeviceIdType.MESH
BF = jnp.bfloat16
F32 = jnp.float32

X_GATHER = 0
RING = 3
TWIN = 15
HALO = 18
SCAN = 20
SWAP = 27
MESSAGES = 30


def kernel(
    tok_hbm, scale_ref, shift_ref, gate_ref, wq_hbm, wk_hbm, wv_hbm, wo_hbm, mix_ref,
    decay_ref, last_ref, list_ref, out_hbm,
    tok, resid, raw, wo_raw, wvk, wq, wo, vbuf, kbuf, qbuf, win, mixb, acc,
    sloc, scur, pack_out, pack_in, mixrep, local_sem, send_sem, recv_sem,
):
    tm = lax.axis_index("tm")
    sp = lax.axis_index("space")
    z, y, core = tm // 8, (tm // 2) % 4, tm % 2

    def at(zz, yy, cc):
        return (zz * 8 + yy * 2 + cc, sp)

    def x_peer(step):
        return (tm, (sp + step) % 4)

    def z_peer(step):
        return at((z + step) % 4, y, core)

    def y_peer(step):
        return at(z, (y + step) % 4, core)

    twin = at(z, y, 1 - core)
    right = ((tm + 1) % 32, sp)
    left = ((tm + 31) % 32, sp)
    outer = ((tm + 31 + 2 * core) % 32, sp)

    def remote(number, src, dst, device):
        return pltpu.make_async_remote_copy(
            src_ref=src,
            dst_ref=dst,
            send_sem=send_sem.at[number],
            recv_sem=recv_sem.at[number],
            device_id=device,
            device_id_type=MESH,
        )

    def load(number, src, dst):
        return pltpu.make_async_copy(src, dst, local_sem.at[number])

    load_wo = load(0, wo_hbm, wo_raw)
    load_wv = load(1, wv_hbm, raw.at[0])
    load_wk = load(2, wk_hbm, raw.at[1])
    load_wq = load(3, wq_hbm, raw.at[0])
    load_resid = load(4, tok_hbm.at[pl.ds(pl.multiple_of(sp * ROWS, ROWS), ROWS)], resid)

    def load_tok(f):
        return load(5 + f, tok_hbm.at[pl.ds(f * ROWS, ROWS)], tok.at[f])

    load_wo.start()
    load_wv.start()
    load_tok(0).start()
    load_wk.start()
    for f in range(1, FR):
        load_tok(f).start()
    load_resid.start()

    barrier = pltpu.get_barrier_semaphore()
    partners = [x_peer(i) for i in (1, 2, 3)] + [y_peer(i) for i in (1, 2, 3)]
    partners += [z_peer(i) for i in (1, 2, 3)] + [twin, outer]
    for device in partners:
        pl.semaphore_signal(barrier, inc=1, device_id=device, device_id_type=MESH)
    pl.semaphore_wait(barrier, len(partners))

    load_wo.wait()
    for h in range(NH):
        wo[0, h, 0:HD, 0:D] = wo_raw[h * HD : (h + 1) * HD, :]
        wo[0, h, HD:HP, 0:D] = jnp.zeros((HP - HD, D), BF)
        wo[0, h, :, D:DP] = jnp.zeros((HP, DP - D), BF)

    def columns(c):
        return pl.ds(pl.multiple_of(c * HALF, HALF), HALF)

    def chunk(p, i, first=0, count=32):
        return wo.at[p, :, pl.ds(pl.multiple_of(i * 32 + first, 16), count), columns(core)]

    def place(p):
        return (y, y_peer) if RELS[p] == 2 else (z, z_peer)

    def x_gather(p):
        i, _ = place(p)
        return remote(X_GATHER + p - 1, chunk(0, i), chunk(p, i), x_peer(4 - RELS[p]))

    def ring(p, k):
        i, peer = place(p)
        below, above = (i + 3) % 4, (i + 1) % 4
        if k == 0:
            ref, device = chunk(p, i), peer(1)
        elif k == 1:
            ref, device = chunk(p, i), peer(3)
        elif k == 2:
            ref, device = chunk(p, below, 0, 16), peer(1)
        else:
            ref, device = chunk(p, above, 16, 16), peer(3)
        return remote(RING + (p - 1) * 4 + k, ref, ref, device)

    def to_twin(p):
        ref = wo.at[p, :, :, columns(core)]
        return remote(TWIN + p - 1, ref, ref, twin)

    def ring_first(p):
        x_gather(p).wait_recv()
        ring(p, 0).start()
        ring(p, 1).start()

    def ring_second(p):
        ring(p, 0).wait_recv()
        ring(p, 1).wait_recv()
        ring(p, 2).start()
        ring(p, 3).start()

    def ring_last(p):
        ring(p, 2).wait_recv()
        ring(p, 3).wait_recv()
        to_twin(p).start()

    for p in (2, 3, 1):
        x_gather(p).start()

    def pad_heads(slot, dst, base):
        rows = 160

        def one(i, _):
            r = pl.ds(pl.multiple_of(i * rows, rows), rows)
            part = raw[slot, r, :]
            for h in range(NH):
                dst[r, base + h * HP : base + (h + 1) * HP] = jnp.concatenate(
                    [part[:, h * HD : (h + 1) * HD], jnp.zeros((rows, HP - HD), BF)], axis=1
                )
            return 0

        lax.fori_loop(0, D // rows, one, 0)

    load_wv.wait()
    pad_heads(0, wvk, 0)
    load_wq.start()
    load_wk.wait()
    pad_heads(1, wvk, GW)
    scur[...] = jnp.zeros_like(scur)

    def norm(f):
        rows = 32

        def one(i, _):
            r = pl.ds(pl.multiple_of(i * rows, rows), rows)
            x = tok[f, r, :].astype(F32)
            inverse = lax.rsqrt(jnp.sum(x * x, axis=-1, keepdims=True) * (1.0 / D) + EPS)
            tok[f, r, :] = (x * inverse * (1.0 + scale_ref[...]) + shift_ref[...]).astype(BF)
            return 0

        lax.fori_loop(0, ROWS // rows, one, 0)

    def halo_left():
        return remote(HALO, vbuf.at[pl.ds(2, 2)], vbuf.at[pl.ds(6, 2)], left)

    def halo_right():
        return remote(HALO + 1, vbuf.at[pl.ds(4, 2)], vbuf.at[pl.ds(0, 2)], right)

    def decay(f, h):
        return jnp.exp(jnp.full((1, HP), decay_ref[f, h], F32))

    def frame(f, _):
        load_tok(f).wait()
        norm(f)
        for n in range(2 * GW // 256):
            part = jnp.dot(
                tok[f], wvk[:, n * 256 : (n + 1) * 256], preferred_element_type=F32
            ).astype(BF)
            for half in range(2):
                piece = part[:, half * HP : (half + 1) * HP]
                at_col = n * 256 + half * HP
                if at_col < GW:
                    vbuf[2 + f, :, at_col : at_col + HP] = piece
                else:
                    kbuf[:, at_col - GW : at_col - GW + HP] = piece
        for h in range(NH):
            cols = slice(h * HP, (h + 1) * HP)
            fresh = lax.dot_general(
                kbuf[:, cols], vbuf[2 + f, :, cols], (((0,), (0,)), ((), ())),
                preferred_element_type=F32,
            )
            state = decay(f, h) * scur[h] + fresh
            scur[h] = state
            sloc[f, h] = state

        @pl.when(f == 1)
        def _():
            halo_left().start()
            ring_first(2)
            ring_first(3)

        @pl.when(f == 2)
        def _():
            ring_first(1)

        @pl.when(f == 3)
        def _():
            halo_right().start()

        return 0

    lax.fori_loop(0, FR, frame, 0)

    row_id = lax.broadcasted_iota(jnp.int32, (HP, HP), 0)

    def pack(slot, h, log, state):
        high = log.astype(BF).astype(F32)
        low = log - high
        body = jnp.where(row_id < HD, state, 0.0)
        body = jnp.where(row_id == HD, high, jnp.where(row_id == HD + 1, low, body))
        pack_out[slot, h] = body.astype(BF)

    def unpack(slot, h):
        body = pack_in[slot, h].astype(F32)
        log = body[HD : HD + 1, :] + body[HD + 1 : HD + 2, :]
        return log, jnp.where(row_id < HD, body, 0.0)

    def flag(condition):
        return jnp.where(condition, 1.0, 0.0).astype(F32)

    def join(early, late):
        return early[0] + late[0], jnp.exp(late[0]) * early[1] + late[1]

    def choose(on, pair, other):
        return tuple(on * a + (1.0 - on) * b for a, b in zip(pair, other))

    def masked(on, pair):
        return tuple(on * a for a in pair)

    def own_pair(h):
        log = jnp.full((1, HP), decay_ref[0, h], F32)
        for f in range(1, FR):
            log = log + jnp.full((1, HP), decay_ref[f, h], F32)
        return log, scur[h]

    first_core = flag(core == 0)

    def chip_pair(h):
        own, other = own_pair(h), unpack(0, h)
        return join(choose(first_core, own, other), choose(first_core, other, own))

    def scan_core():
        return remote(SCAN, pack_out.at[0], pack_in.at[0], twin)

    def scan_y(step):
        return remote(SCAN + step, pack_out.at[1], pack_in.at[step], y_peer(step))

    def scan_z(step):
        return remote(SCAN + 3 + step, pack_out.at[2], pack_in.at[3 + step], z_peer(step))

    def row_prefix(h):
        total = None
        for step in (3, 2, 1):
            pair = masked(flag(y >= step), unpack(step, h))
            total = pair if total is None else join(total, pair)
        return total

    def column_prefix(h):
        total = None
        for step in (3, 2, 1):
            pair = masked(flag(z >= step), unpack(3 + step, h))
            total = pair if total is None else join(total, pair)
        return total

    for h in range(NH):
        pack(0, h, *own_pair(h))
    scan_core().start()

    load_wq.wait()
    pad_heads(0, wq, 0)

    def query(f, _):
        for n in range(3):
            width = 256 if n < 2 else 128
            cols = slice(n * 256, n * 256 + width)
            qbuf[f, :, cols] = jnp.dot(
                tok[f], wq[:, cols], preferred_element_type=F32
            ).astype(BF)
        return 0

    scan_core().wait_recv()
    for h in range(NH):
        pack(1, h, *chip_pair(h))
    for step in (1, 2, 3):
        scan_y(step).start()

    lax.fori_loop(0, 2, query, 0)
    ring_second(2)
    ring_second(3)

    for step in (1, 2, 3):
        scan_y(step).wait_recv()
    for h in range(NH):
        total = join(row_prefix(h), chip_pair(h))
        for step in (3, 2, 1):
            total = join(total, masked(flag(y < step), unpack(step, h)))
        pack(2, h, *total)
    for step in (1, 2, 3):
        scan_z(step).start()

    lax.fori_loop(2, FR, query, 0)
    ring_second(1)

    lane = lax.broadcasted_iota(jnp.int32, (TT, HP), 1)
    spread = jnp.where(lane % TT == lax.broadcasted_iota(jnp.int32, (TT, HP), 0), 1.0, 0.0)
    mixrep[...] = jnp.dot(mix_ref[...], spread.astype(BF), preferred_element_type=F32)
    group = lane // TT + (FR * tm - WIN)
    halo_left().wait_recv()
    halo_right().wait_recv()

    def tile(j, _):
        r = pl.ds(pl.multiple_of(j * TT, TT), TT)
        blocks = []
        for f in range(FR):
            block = jnp.zeros((TT, HP), F32)
            for n in range(NBR):
                hit = group == list_ref[(f * TILES + j) * NBR + n]
                block = block + jnp.where(hit, mixrep[n * TT : (n + 1) * TT, :], 0.0)
            blocks.append(block)
        matrix = jnp.concatenate(blocks, axis=0).astype(BF)
        source = vbuf[:, r, :].reshape(2 * FR * TT, GW)
        mixed = jnp.dot(matrix, source, preferred_element_type=F32).astype(BF)
        win[:, r, :] = mixed.reshape(FR, TT, GW)
        return 0

    lax.fori_loop(0, TILES, tile, 0)

    for step in (1, 2, 3):
        scan_z(step).wait_recv()
    for h in range(NH):
        chip = masked(1.0 - first_core, unpack(0, h))
        entering = join(join(column_prefix(h), row_prefix(h)), chip)[1]
        for f in range(FR):
            entering = decay(f, h) * entering
            sloc[f, h] = sloc[f, h] + entering

    def swap(p):
        f = (sp + 4 - RELS[p]) % 4
        return remote(
            SWAP + p - 1, qbuf.at[f], mixb.at[:, pl.ds(p * GW, GW)], x_peer(4 - RELS[p])
        )

    for p in (1, 2, 3, 0):
        f = (sp + 4 - RELS[p]) % 4
        for h in range(NH):
            cols = slice(h * HP, (h + 1) * HP)
            state = jnp.zeros((HP, HP), F32)
            for g in range(FR):
                state = state + flag(last_ref[f] == FR * tm + g) * sloc[g, h]
            state = state.astype(BF)
            for half in range(2):
                r = slice(half * 256, (half + 1) * 256)
                linear = jnp.dot(qbuf[f, r, cols], state, preferred_element_type=F32)
                inverse = lax.rsqrt(
                    jnp.sum(linear * linear, axis=-1, keepdims=True) * (1.0 / HD) + EPS
                )
                both = (linear * inverse + win[f, r, cols].astype(F32)).astype(BF)
                if p == 0:
                    mixb[r, cols] = both
                else:
                    qbuf[f, r, cols] = both
        if p > 0:
            swap(p).start()
        if p == 1:
            ring_last(2)
        if p == 2:
            ring_last(3)
        if p == 3:
            ring_last(1)

    load_resid.wait()
    to_twin(1).wait_recv()
    swap(1).wait_recv()

    def weights(p, cols, width):
        return wo[p : p + 2, :, :, cols].reshape(2 * GW, width)

    def first_part(n, _):
        cols = pl.ds(pl.multiple_of(n * 256, 256), 256)
        acc[:, cols] = jnp.dot(
            mixb[:, 0 : 2 * GW], weights(0, cols, 256), preferred_element_type=F32
        )
        return 0

    lax.fori_loop(0, DP // 256, first_part, 0)

    for p in (2, 3):
        to_twin(p).wait_recv()
        swap(p).wait_recv()

    def finish(cols, width):
        total = acc[:, cols] + jnp.dot(
            mixb[:, 2 * GW : 4 * GW], weights(2, cols, width), preferred_element_type=F32
        )
        resid[:, cols] = (resid[:, cols].astype(F32) + gate_ref[:, cols] * total).astype(BF)

    def second_part(n, _):
        finish(pl.ds(pl.multiple_of(n * 256, 256), 256), 256)
        return 0

    lax.fori_loop(0, D // 256, second_part, 0)
    finish(slice(D // 256 * 256, D), D % 256)
    store = load(9, resid, out_hbm)
    store.start()

    for p in (1, 2, 3):
        x_gather(p).wait_send()
        for k in range(4):
            ring(p, k).wait_send()
        to_twin(p).wait_send()
        swap(p).wait_send()
        scan_y(p).wait_send()
        scan_z(p).wait_send()
    scan_core().wait_send()
    halo_left().wait_send()
    halo_right().wait_send()
    store.wait()


def body(
    tokens, mod_scale, mod_shift, out_gate, w_query, w_key, w_value, w_out,
    log_decay, mix_weight, block_last, win_list,
):
    lists = lax.dynamic_slice_in_dim(win_list, lax.axis_index("tm") * FR, FR, 0).reshape(-1)
    anywhere = pl.BlockSpec(memory_space=pl.ANY)
    vmem = pl.BlockSpec(memory_space=pltpu.VMEM)
    smem = pl.BlockSpec(memory_space=pltpu.SMEM)
    return pl.pallas_call(
        kernel,
        out_shape=jax.ShapeDtypeStruct((ROWS, D), BF),
        in_specs=[anywhere, vmem, vmem, vmem] + [anywhere] * 4 + [vmem, smem, smem, smem],
        out_specs=anywhere,
        scratch_shapes=[
            pltpu.VMEM((FR, ROWS, D), BF),
            pltpu.VMEM((ROWS, D), BF),
            pltpu.VMEM((2, D, NH * HD), BF),
            pltpu.VMEM((NH * HD, D), BF),
            pltpu.VMEM((D, 2 * GW), BF),
            pltpu.VMEM((D, GW), BF),
            pltpu.VMEM((4, NH, HP, DP), BF),
            pltpu.VMEM((2 * FR, ROWS, GW), BF),
            pltpu.VMEM((ROWS, GW), BF),
            pltpu.VMEM((FR, ROWS, GW), BF),
            pltpu.VMEM((FR, ROWS, GW), BF),
            pltpu.VMEM((ROWS, 4 * GW), BF),
            pltpu.VMEM((ROWS, DP), F32),
            pltpu.VMEM((FR, NH, HP, HP), F32),
            pltpu.VMEM((NH, HP, HP), F32),
            pltpu.VMEM((3, NH, HP, HP), BF),
            pltpu.VMEM((7, NH, HP, HP), BF),
            pltpu.VMEM((NBR * TT, HP), F32),
            pltpu.SemaphoreType.DMA((10,)),
            pltpu.SemaphoreType.DMA((MESSAGES,)),
            pltpu.SemaphoreType.DMA((MESSAGES,)),
        ],
        compiler_params=pltpu.CompilerParams(
            collective_id=0, has_side_effects=True, vmem_limit_bytes=66_000_000
        ),
    )(
        tokens,
        mod_scale.reshape(1, D),
        mod_shift.reshape(1, D),
        out_gate.reshape(1, D),
        w_query,
        w_key,
        w_value,
        w_out,
        mix_weight.reshape(NBR * TT, TT),
        log_decay,
        block_last,
        lists,
    )


def solution(mesh):
    placed = (
        P("tm", None),
        P(),
        P(),
        P(),
        P(None, "space"),
        P(None, "space"),
        P(None, "space"),
        P("space", None),
        P("tm", "space"),
        P(),
        P("tm"),
        P(),
    )
    return jax.shard_map(
        body, mesh=mesh, in_specs=placed, out_specs=P(("tm", "space"), None), check_vma=False
    )
```

```python
import jax
import jax.numpy as jnp
from jax import lax
from jax.experimental import pallas as pl
from jax.experimental.pallas import tpu as pltpu
from jax.sharding import PartitionSpec as P

HD = 112
NH = 5
GW = NH * HD
GP = 640
D = 2240
FR = 4
ROWS = 512
TILES = 32
TT = 16
NBR = 8
WIN = 2
PART = 288
EPS = 1e-06
RELS = (0, 2, 3, 1)
MESH = pl.DeviceIdType.MESH
BF = jnp.bfloat16
F32 = jnp.float32
NT = (((1,), (1,)), ((), ()))

X_GATHER = 0
RING = 3
TWIN = 15
HALO = 18
SCAN = 20
SWAP = 27
MESSAGES = 30


def kernel(
    tok_hbm, scale_ref, shift_ref, gate_ref, wq_hbm, wk_hbm, wv_hbm, wo_hbm, mix_ref,
    decay_ref, last_ref, list_ref, out_hbm,
    tok, resid, wqkv, wo_raw, wo, vbuf, kbuf, qbuf, win, mixb, acc, gains,
    sloc, scur, pack_out, pack_in, mixrep, rel, band, local_sem, send_sem, recv_sem,
):
    tm = lax.axis_index("tm")
    sp = lax.axis_index("space")
    z, y, core = tm // 8, (tm // 2) % 4, tm % 2

    def at(zz, yy, cc):
        return (zz * 8 + yy * 2 + cc, sp)

    def x_peer(step):
        return (tm, (sp + step) % 4)

    def z_peer(step):
        return at((z + step) % 4, y, core)

    def y_peer(step):
        return at(z, (y + step) % 4, core)

    twin = at(z, y, 1 - core)
    right = ((tm + 1) % 32, sp)
    left = ((tm + 31) % 32, sp)
    outer = ((tm + 31 + 2 * core) % 32, sp)

    def remote(number, src, dst, device):
        return pltpu.make_async_remote_copy(
            src_ref=src,
            dst_ref=dst,
            send_sem=send_sem.at[number],
            recv_sem=recv_sem.at[number],
            device_id=device,
            device_id_type=MESH,
        )

    def load(number, src, dst):
        return pltpu.make_async_copy(src, dst, local_sem.at[number])

    load_wo = load(0, wo_hbm, wo_raw.at[pl.ds(0, GW)])
    load_wv = load(1, wv_hbm, wqkv.at[0])
    load_wk = load(2, wk_hbm, wqkv.at[1])
    load_wq = load(3, wq_hbm, wqkv.at[2])
    own_rows = pl.ds(pl.multiple_of(sp * ROWS, ROWS), ROWS)
    load_resid = load(4, tok_hbm.at[:, own_rows], resid)

    def load_tok(f):
        rows = pl.ds(pl.multiple_of(f * ROWS, ROWS), ROWS)
        return load(5 + f, tok_hbm.at[:, rows], tok.at[f])

    load_wo.start()
    load_tok(0).start()
    load_wv.start()
    for f in range(1, FR):
        load_tok(f).start()
    load_wk.start()
    load_wq.start()
    load_resid.start()

    barrier = pltpu.get_barrier_semaphore()
    partners = [x_peer(i) for i in (1, 2, 3)] + [y_peer(i) for i in (1, 2, 3)]
    partners += [z_peer(i) for i in (1, 2, 3)] + [twin, outer]
    for device in partners:
        pl.semaphore_signal(barrier, inc=1, device_id=device, device_id_type=MESH)

    for k, vector in enumerate((scale_ref, shift_ref, gate_ref)):
        for low in range(0, D, 128):
            high = min(low + 128, D)
            row = vector[pl.ds(low, high - low)].reshape(1, high - low)
            column = jnp.broadcast_to(row, (128, high - low)).T
            gains[k, low:high, :] = 1.0 + column if k == 0 else column

    def spots(rows, lanes, of_row, of_lane):
        r = lax.broadcasted_iota(jnp.int32, (rows, lanes), 0)
        l = lax.broadcasted_iota(jnp.int32, (rows, lanes), 1)
        return jnp.where(of_row(r) == of_lane(l), 1.0, 0.0).astype(BF)

    def exact(a, b, dims=(((1,), (0,)), ((), ()))):
        return lax.dot_general(a, b, dims, preferred_element_type=F32)

    mixed_t = exact(spots(TT, TT, lambda r: r, lambda l: l), mix_ref[...], NT).astype(BF)
    mine = exact(
        spots(8, 128, lambda r: r + FR * tm, lambda l: l), list_ref[...].astype(BF), NT
    )
    mine = (mine - (FR * tm - WIN).astype(F32)).astype(BF)
    for n in range(NBR):
        mixrep[n] = exact(
            mixed_t, spots(128, 128, lambda r: r, lambda l: l % TT + n * TT)
        )
        rel[n] = exact(
            mine, spots(TILES * NBR, ROWS, lambda r: r, lambda l: l // TT * NBR + n)
        )
    band[...] = jnp.zeros_like(band)
    for p in range(4):
        mixb[p * GP + GW : (p + 1) * GP, :] = jnp.zeros((GP - GW, ROWS), BF)

    wo_raw[GW:GP, :] = jnp.zeros((GP - GW, D), BF)
    wo[3, 1, D - 7 * PART : PART, 0:GP] = jnp.zeros((8 * PART - D, GP), BF)
    load_wo.wait()
    for low in range(0, D, 256):
        high = min(low + 256, D)
        eye = spots(high - low, high - low, lambda r: r, lambda l: l)
        turned = exact(eye, wo_raw[:, low:high], NT).astype(BF)
        for part in range(8):
            first, last = max(low, part * PART), min(high, (part + 1) * PART)
            if first < last:
                wo[part // 2, part % 2, first - part * PART : last - part * PART, 0:GP] = turned[
                    first - low : last - low
                ]

    pl.semaphore_wait(barrier, len(partners))

    def chunk(p, i, first=0, count=PART):
        return wo.at[i, core, pl.ds(first, count), pl.ds(p * GP, GP)]

    def place(p):
        return (y, y_peer) if RELS[p] == 2 else (z, z_peer)

    def x_gather(p):
        i, _ = place(p)
        return remote(X_GATHER + p - 1, chunk(0, i), chunk(p, i), x_peer(4 - RELS[p]))

    def ring(p, k):
        i, peer = place(p)
        below, above = (i + 3) % 4, (i + 1) % 4
        if k == 0:
            ref, device = chunk(p, i), peer(1)
        elif k == 1:
            ref, device = chunk(p, i), peer(3)
        elif k == 2:
            ref, device = chunk(p, below, 0, PART // 2), peer(1)
        else:
            ref, device = chunk(p, above, PART // 2, PART // 2), peer(3)
        return remote(RING + (p - 1) * 4 + k, ref, ref, device)

    def to_twin(p):
        ref = wo.at[:, core, :, pl.ds(p * GP, GP)]
        return remote(TWIN + p - 1, ref, ref, twin)

    def ring_first(p):
        x_gather(p).wait_recv()
        ring(p, 0).start()
        ring(p, 1).start()

    def ring_second(p):
        ring(p, 0).wait_recv()
        ring(p, 1).wait_recv()
        ring(p, 2).start()
        ring(p, 3).start()

    def ring_last(p):
        ring(p, 2).wait_recv()
        ring(p, 3).wait_recv()
        to_twin(p).start()

    for p in (2, 3, 1):
        x_gather(p).start()

    def norm(f):
        rows = 32

        def squares(i, total):
            x = tok[f, pl.ds(pl.multiple_of(i * rows, rows), rows), :].astype(F32)
            return total + jnp.sum((x * x).reshape(rows // 8, 8, ROWS), axis=0)

        total = lax.fori_loop(0, D // rows, squares, jnp.zeros((8, ROWS), F32), unroll=2)
        inverse = lax.rsqrt(jnp.sum(total, axis=0, keepdims=True) * (1.0 / D) + EPS)

        def scale(i, _):
            r = pl.ds(pl.multiple_of(i * rows, rows), rows)
            gain, shift = gains[0, r, :], gains[1, r, :]
            for c in range(ROWS // 128):
                cols = slice(c * 128, (c + 1) * 128)
                x = tok[f, r, cols].astype(F32)
                tok[f, r, cols] = (x * inverse[:, cols] * gain + shift).astype(BF)
            return 0

        lax.fori_loop(0, D // rows, scale, 0, unroll=2)

    def halo_left():
        return remote(HALO, vbuf.at[pl.ds(2, 2)], vbuf.at[pl.ds(6, 2)], left)

    def halo_right():
        return remote(HALO + 1, vbuf.at[pl.ds(4, 2)], vbuf.at[pl.ds(0, 2)], right)

    def decay(f, h):
        return jnp.exp(jnp.full((1, HD), decay_ref[f, h], F32))

    def project(weight, f, dst):
        for half in range(2):
            cols = slice(half * 256, (half + 1) * 256)
            dst[:, cols] = jnp.dot(
                wqkv[weight], tok[f, :, cols], preferred_element_type=F32
            ).astype(BF)

    load_wv.wait()

    def value(f, _):
        load_tok(f).wait()
        norm(f)
        project(0, f, vbuf.at[2 + f])

        @pl.when(f == 1)
        def _():
            halo_left().start()

        @pl.when(f == 3)
        def _():
            halo_right().start()

        return 0

    lax.fori_loop(0, FR, value, 0)
    ring_first(2)
    ring_first(3)

    load_wk.wait()
    scur[...] = jnp.zeros_like(scur)

    def key(f, _):
        project(1, f, kbuf)
        for h in range(NH):
            rows = slice(h * HD, (h + 1) * HD)
            fresh = exact(vbuf[2 + f, rows, :], kbuf[rows, :], NT)
            state = decay(f, h) * scur[h] + fresh
            scur[h] = state
            sloc[f, h] = state
        return 0

    lax.fori_loop(0, FR, key, 0)

    row_id = lax.broadcasted_iota(jnp.int32, (TT, HD), 0)

    def pack(slot, h, log, state):
        high = log.astype(BF).astype(F32)
        low = log - high
        tail = jnp.where(row_id == 0, high, jnp.where(row_id == 1, low, 0.0))
        pack_out[slot, h, 0:HD, :] = state.astype(BF)
        pack_out[slot, h, HD:128, :] = tail.astype(BF)

    def unpack(slot, h):
        tail = pack_in[slot, h, HD:128, :].astype(F32)
        return jnp.sum(tail, axis=0, keepdims=True), pack_in[slot, h, 0:HD, :].astype(F32)

    def flag(condition):
        return jnp.where(condition, 1.0, 0.0).astype(F32)

    def join(early, late):
        return early[0] + late[0], jnp.exp(late[0]) * early[1] + late[1]

    def choose(on, pair, other):
        return tuple(on * a + (1.0 - on) * b for a, b in zip(pair, other))

    def masked(on, pair):
        return tuple(on * a for a in pair)

    def own_pair(h):
        log = jnp.full((1, HD), decay_ref[0, h], F32)
        for f in range(1, FR):
            log = log + jnp.full((1, HD), decay_ref[f, h], F32)
        return log, scur[h]

    first_core = flag(core == 0)

    def chip_pair(h):
        own, other = own_pair(h), unpack(0, h)
        return join(choose(first_core, own, other), choose(first_core, other, own))

    def scan_core():
        return remote(SCAN, pack_out.at[0], pack_in.at[0], twin)

    def scan_y(step):
        return remote(SCAN + step, pack_out.at[1], pack_in.at[step], y_peer(step))

    def scan_z(step):
        return remote(SCAN + 3 + step, pack_out.at[2], pack_in.at[3 + step], z_peer(step))

    def row_prefix(h):
        total = None
        for step in (3, 2, 1):
            pair = masked(flag(y >= step), unpack(step, h))
            total = pair if total is None else join(total, pair)
        return total

    def column_prefix(h):
        total = None
        for step in (3, 2, 1):
            pair = masked(flag(z >= step), unpack(3 + step, h))
            total = pair if total is None else join(total, pair)
        return total

    for h in range(NH):
        pack(0, h, *own_pair(h))
    scan_core().start()

    load_wq.wait()

    def query(f, _):
        project(2, f, qbuf.at[f])
        return 0

    ring_first(1)
    scan_core().wait_recv()
    for h in range(NH):
        pack(1, h, *chip_pair(h))
    for step in (1, 2, 3):
        scan_y(step).start()

    lax.fori_loop(0, 2, query, 0)
    ring_second(2)
    ring_second(3)

    for step in (1, 2, 3):
        scan_y(step).wait_recv()
    for h in range(NH):
        total = join(row_prefix(h), chip_pair(h))
        for step in (3, 2, 1):
            total = join(total, masked(flag(y < step), unpack(step, h)))
        pack(2, h, *total)
    for step in (1, 2, 3):
        scan_z(step).start()

    lax.fori_loop(2, FR, query, 0)
    ring_second(1)

    halo_left().wait_recv()
    halo_right().wait_recv()
    tile_of_lane = lax.broadcasted_iota(jnp.int32, (TT, 128), 1) // TT

    def tiles(j, _):
        cols = pl.ds(pl.multiple_of(j * 128, 128), 128)
        for pair in range(2):
            for f in range(2):
                for g in range(f, f + 2 * WIN + 1):
                    block = jnp.zeros((TT, 128), F32)
                    for n in range(NBR):
                        listed = rel[n, pl.ds(2 * pair + f, 1), cols]
                        block = block + jnp.where(listed == 2 * pair + g, mixrep[n], 0.0)
                    for t in range(8):
                        low = g * 128 + t * TT
                        band[pair, low : low + TT, f * 128 : (f + 1) * 128] = jnp.where(
                            tile_of_lane == t, block, 0.0
                        ).astype(BF)
            source = jnp.concatenate(
                [vbuf[2 * pair + g, :, cols] for g in range(2 * WIN + 2)], axis=1
            )
            mixed = exact(source, band[pair]).astype(BF)
            for f in range(2):
                win[2 * pair + f, :, cols] = mixed[:, f * 128 : (f + 1) * 128]
        return 0

    lax.fori_loop(0, ROWS // 128, tiles, 0)

    for step in (1, 2, 3):
        scan_z(step).wait_recv()
    for h in range(NH):
        chip = masked(1.0 - first_core, unpack(0, h))
        entering = join(join(column_prefix(h), row_prefix(h)), chip)[1]
        for f in range(FR):
            entering = decay(f, h) * entering
            sloc[f, h] = sloc[f, h] + entering

    def swap(p):
        f = (sp + 4 - RELS[p]) % 4
        return remote(
            SWAP + p - 1, qbuf.at[f], mixb.at[pl.ds(p * GP, GW)], x_peer(4 - RELS[p])
        )

    for p in (1, 2, 3, 0):
        f = (sp + 4 - RELS[p]) % 4
        for h in range(NH):
            rows = slice(h * HD, (h + 1) * HD)
            state = jnp.zeros((HD, HD), F32)
            for g in range(FR):
                state = state + flag(last_ref[f] == FR * tm + g) * sloc[g, h]
            linear = exact(state.astype(BF), qbuf[f, rows, :])
            inverse = lax.rsqrt(
                jnp.sum(linear * linear, axis=0, keepdims=True) * (1.0 / HD) + EPS
            )
            both = (linear * inverse + win[f, rows, :].astype(F32)).astype(BF)
            if p == 0:
                mixb[rows, :] = both
            else:
                qbuf[f, rows, :] = both
        if p > 0:
            swap(p).start()
        if p == 1:
            ring_last(2)
        if p == 2:
            ring_last(3)
        if p == 3:
            ring_last(1)

    load_resid.wait()

    def weights(i, p, count):
        return wo[i, :, :, p * GP : (p + count) * GP].reshape(2 * PART, count * GP)

    for i in range(4):
        low, high = i * 2 * PART, min((i + 1) * 2 * PART, D)
        acc[low:high, :] = exact(weights(i, 0, 1)[: high - low], mixb[0:GP, :])

    to_twin(1).wait_recv()
    swap(1).wait_recv()
    for i in range(4):
        low, high = i * 2 * PART, min((i + 1) * 2 * PART, D)
        acc[low:high, :] += exact(weights(i, 1, 1)[: high - low], mixb[GP : 2 * GP, :])

    for p in (2, 3):
        to_twin(p).wait_recv()
        swap(p).wait_recv()
    for i in range(4):
        low, high = i * 2 * PART, min((i + 1) * 2 * PART, D)
        total = acc[low:high, :] + exact(weights(i, 2, 2)[: high - low], mixb[2 * GP : 4 * GP, :])
        for c in range(ROWS // 128):
            cols = slice(c * 128, (c + 1) * 128)
            resid[low:high, cols] = (
                resid[low:high, cols].astype(F32) + gains[2, low:high, :] * total[:, cols]
            ).astype(BF)
    store = load(9, resid, out_hbm)
    store.start()

    for p in (1, 2, 3):
        x_gather(p).wait_send()
        for k in range(4):
            ring(p, k).wait_send()
        to_twin(p).wait_send()
        swap(p).wait_send()
        scan_y(p).wait_send()
        scan_z(p).wait_send()
    scan_core().wait_send()
    halo_left().wait_send()
    halo_right().wait_send()
    store.wait()


def body(
    tokens, mod_scale, mod_shift, out_gate, w_query, w_key, w_value, w_out,
    log_decay, mix_weight, block_last, win_list,
):
    anywhere = pl.BlockSpec(memory_space=pl.ANY)
    vmem = pl.BlockSpec(memory_space=pltpu.VMEM)
    smem = pl.BlockSpec(memory_space=pltpu.SMEM)
    out = pl.pallas_call(
        kernel,
        out_shape=jax.ShapeDtypeStruct((D, ROWS), BF),
        in_specs=[anywhere, vmem, vmem, vmem] + [anywhere] * 4 + [vmem, smem, smem, vmem],
        out_specs=anywhere,
        scratch_shapes=[
            pltpu.VMEM((FR, D, ROWS), BF),
            pltpu.VMEM((D, ROWS), BF),
            pltpu.VMEM((3, GW, D), BF),
            pltpu.VMEM((GP, D), BF),
            pltpu.VMEM((4, 2, PART, 4 * GP), BF),
            pltpu.VMEM((2 * FR, GW, ROWS), BF),
            pltpu.VMEM((GW, ROWS), BF),
            pltpu.VMEM((FR, GW, ROWS), BF),
            pltpu.VMEM((FR, GW, ROWS), BF),
            pltpu.VMEM((4 * GP, ROWS), BF),
            pltpu.VMEM((D, ROWS), F32),
            pltpu.VMEM((3, D, 128), F32),
            pltpu.VMEM((FR, NH, HD, HD), F32),
            pltpu.VMEM((NH, HD, HD), F32),
            pltpu.VMEM((3, NH, 128, HD), BF),
            pltpu.VMEM((7, NH, 128, HD), BF),
            pltpu.VMEM((NBR, TT, 128), F32),
            pltpu.VMEM((NBR, 8, ROWS), F32),
            pltpu.VMEM((2, (2 * WIN + 2) * 128, 256), BF),
            pltpu.SemaphoreType.DMA((10,)),
            pltpu.SemaphoreType.DMA((MESSAGES,)),
            pltpu.SemaphoreType.DMA((MESSAGES,)),
        ],
        compiler_params=pltpu.CompilerParams(
            collective_id=0, has_side_effects=True, vmem_limit_bytes=66_000_000
        ),
    )(
        tokens.T,
        mod_scale,
        mod_shift,
        out_gate,
        w_query.T,
        w_key.T,
        w_value.T,
        w_out,
        mix_weight.reshape(NBR * TT, TT),
        log_decay,
        block_last,
        win_list.transpose(1, 2, 0).reshape(TILES * NBR, -1),
    )
    return out.T


def solution(mesh):
    placed = (
        P("tm", None),
        P(),
        P(),
        P(),
        P(None, "space"),
        P(None, "space"),
        P(None, "space"),
        P("space", None),
        P("tm", "space"),
        P(),
        P("tm"),
        P(),
    )
    return jax.shard_map(
        body, mesh=mesh, in_specs=placed, out_specs=P(("tm", "space"), None), check_vma=False
    )
```

```python
import jax
import jax.numpy as jnp
from jax import lax
from jax.experimental import pallas as pl
from jax.experimental.pallas import tpu as pltpu
from jax.sharding import PartitionSpec as P

HD = 112
NH = 5
GW = NH * HD
GP = 640
D = 2240
FR = 4
ROWS = 512
TILES = 32
TT = 16
NBR = 8
WIN = 2
PART = 288
EPS = 1e-06
RELS = (0, 2, 3, 1)
MESH = pl.DeviceIdType.MESH
BF = jnp.bfloat16
F32 = jnp.float32
NT = (((1,), (1,)), ((), ()))

X_GATHER = 0
RING = 5
TWIN = 13
HALO = 16
SCAN = 18
SWAP = 26
MESSAGES = 29
HALF = 64


def kernel(
    tok_hbm, scale_ref, shift_ref, gate_ref, wq_hbm, wk_hbm, wv_hbm, wo_hbm, mix_ref,
    decay_ref, last_ref, list_ref, out_hbm,
    tok, resid, wqkv, wo_raw, wo, vbuf, kbuf, qbuf, win, mixb, acc, gains,
    sloc, scur, entry, full_out, full_in, half_out, half_in, end_out, end_in,
    mixrep, rel, band, local_sem, send_sem, recv_sem,
):
    tm = lax.axis_index("tm")
    sp = lax.axis_index("space")
    z, y, core = tm // 8, (tm // 2) % 4, tm % 2

    def at(zz, yy, cc):
        return (zz * 8 + yy * 2 + cc, sp)

    def x_peer(step):
        return (tm, (sp + step) % 4)

    def z_peer(step):
        return at((z + step) % 4, y, core)

    def y_peer(step):
        return at(z, (y + step) % 4, core)

    twin = at(z, y, 1 - core)
    right = ((tm + 1) % 32, sp)
    left = ((tm + 31) % 32, sp)
    outer = ((tm + 31 + 2 * core) % 32, sp)

    def remote(number, src, dst, device):
        return pltpu.make_async_remote_copy(
            src_ref=src,
            dst_ref=dst,
            send_sem=send_sem.at[number],
            recv_sem=recv_sem.at[number],
            device_id=device,
            device_id_type=MESH,
        )

    def load(number, src, dst):
        return pltpu.make_async_copy(src, dst, local_sem.at[number])

    load_wo = load(0, wo_hbm, wo_raw.at[pl.ds(0, GW)])
    load_wv = load(1, wv_hbm, wqkv.at[0])
    load_wk = load(2, wk_hbm, wqkv.at[1])
    load_wq = load(3, wq_hbm, wqkv.at[2])
    own_rows = pl.ds(pl.multiple_of(sp * ROWS, ROWS), ROWS)
    load_resid = load(4, tok_hbm.at[:, own_rows], resid)

    def load_tok(f):
        rows = pl.ds(pl.multiple_of(f * ROWS, ROWS), ROWS)
        return load(5 + f, tok_hbm.at[:, rows], tok.at[f])

    load_wo.start()
    load_tok(0).start()
    load_wv.start()
    for f in range(1, FR):
        load_tok(f).start()
    load_wk.start()
    load_wq.start()
    load_resid.start()

    barrier = pltpu.get_barrier_semaphore()
    partners = [x_peer(i) for i in (1, 2, 3)] + [y_peer(i) for i in (1, 2, 3)]
    partners += [z_peer(i) for i in (1, 2, 3)] + [twin, outer]
    for device in partners:
        pl.semaphore_signal(barrier, inc=1, device_id=device, device_id_type=MESH)

    def spots(rows, lanes, of_row, of_lane):
        r = lax.broadcasted_iota(jnp.int32, (rows, lanes), 0)
        l = lax.broadcasted_iota(jnp.int32, (rows, lanes), 1)
        return jnp.where(of_row(r) == of_lane(l), 1.0, 0.0).astype(BF)

    def exact(a, b, dims=(((1,), (0,)), ((), ()))):
        return lax.dot_general(a, b, dims, preferred_element_type=F32)

    for p in range(4):
        mixb[p * GP + GW : (p + 1) * GP, :] = jnp.zeros((GP - GW, ROWS), BF)

    wo_raw[GW:GP, :] = jnp.zeros((GP - GW, D), BF)
    wo[3, 1, D - 7 * PART : PART, 0:GP] = jnp.zeros((8 * PART - D, GP), BF)
    load_wo.wait()
    for low in range(0, D, 256):
        high = min(low + 256, D)
        eye = spots(high - low, high - low, lambda r: r, lambda l: l)
        turned = exact(eye, wo_raw[:, low:high], NT).astype(BF)
        for part in range(8):
            first, last = max(low, part * PART), min(high, (part + 1) * PART)
            if first < last:
                wo[part // 2, part % 2, first - part * PART : last - part * PART, 0:GP] = turned[
                    first - low : last - low
                ]

    pl.semaphore_wait(barrier, len(partners))

    def chunk(p, i, first=0, count=PART):
        return wo.at[i, core, pl.ds(first, count), pl.ds(p * GP, GP)]

    def x_gather(p, second=0):
        i = y if p == 1 else (z + second) % 4
        number = X_GATHER + p - 1 + 2 * second
        return remote(number, chunk(0, i), chunk(p, i), x_peer(4 - RELS[p]))

    def y_ring(k):
        below, above = (y + 3) % 4, (y + 1) % 4
        if k == 0:
            ref, device = chunk(1, y), y_peer(1)
        elif k == 1:
            ref, device = chunk(1, y), y_peer(3)
        elif k == 2:
            ref, device = chunk(1, below, 0, PART // 2), y_peer(1)
        else:
            ref, device = chunk(1, above, PART // 2, PART // 2), y_peer(3)
        return remote(RING + k, ref, ref, device)

    def z_pass(p, second):
        ref = chunk(p, (z + second) % 4)
        return remote(RING + 4 + (p - 2) * 2 + second, ref, ref, z_peer(3 if second else 1))

    def to_twin(p):
        ref = wo.at[:, core, :, pl.ds(p * GP, GP)]
        return remote(TWIN + p - 1, ref, ref, twin)

    for p in (2, 3, 1):
        x_gather(p).start()
    for p in (2, 3):
        x_gather(p, 1).start()

    parts = []
    for vector in (1.0 + scale_ref[...], shift_ref[...], gate_ref[...]):
        rest = vector.reshape(1, D)
        for _ in range(3):
            part = rest.astype(BF)
            parts.append(part)
            rest = rest - part.astype(F32)
    parts = jnp.concatenate(parts + [jnp.zeros((7, D), BF)], axis=0)
    gains[...] = exact(
        parts, spots(16, 384, lambda r: r // 3, lambda l: l // 128), (((0,), (0,)), ((), ()))
    )

    def norm(f):
        rows = 32

        def squares(i, total):
            x = tok[f, pl.ds(pl.multiple_of(i * rows, rows), rows), :].astype(F32)
            return total + jnp.sum((x * x).reshape(rows // 8, 8, ROWS), axis=0)

        total = lax.fori_loop(0, D // rows, squares, jnp.zeros((8, ROWS), F32), unroll=2)
        inverse = lax.rsqrt(jnp.sum(total, axis=0, keepdims=True) * (1.0 / D) + EPS)

        def scale(i, _):
            r = pl.ds(pl.multiple_of(i * rows, rows), rows)
            gain, shift = gains[r, 0:128], gains[r, 128:256]
            for c in range(ROWS // 128):
                cols = slice(c * 128, (c + 1) * 128)
                x = tok[f, r, cols].astype(F32)
                tok[f, r, cols] = (x * inverse[:, cols] * gain + shift).astype(BF)
            return 0

        lax.fori_loop(0, D // rows, scale, 0, unroll=2)

    def halo_left():
        return remote(HALO, vbuf.at[pl.ds(2, 2)], vbuf.at[pl.ds(6, 2)], left)

    def halo_right():
        return remote(HALO + 1, vbuf.at[pl.ds(4, 2)], vbuf.at[pl.ds(0, 2)], right)

    def decay(f, h):
        return jnp.exp(jnp.full((1, HD), decay_ref[f, h], F32))

    def project(weight, f, dst):
        for half in range(2):
            cols = slice(half * 256, (half + 1) * 256)
            dst[:, cols] = jnp.dot(
                wqkv[weight], tok[f, :, cols], preferred_element_type=F32
            ).astype(BF)

    load_wv.wait()

    def value(f, _):
        load_tok(f).wait()
        norm(f)
        project(0, f, vbuf.at[2 + f])

        @pl.when(f == 1)
        def _():
            halo_left().start()
            for p in (2, 3):
                x_gather(p).wait_recv()
                z_pass(p, 0).start()

        @pl.when(f == 2)
        def _():
            x_gather(1).wait_recv()
            y_ring(0).start()
            y_ring(1).start()

        @pl.when(f == 3)
        def _():
            halo_right().start()
            for p in (2, 3):
                x_gather(p, 1).wait_recv()
                z_pass(p, 1).start()

        return 0

    lax.fori_loop(0, FR, value, 0)

    load_wk.wait()
    scur[...] = jnp.zeros_like(scur)

    def key(f, _):
        project(1, f, kbuf)
        for h in range(NH):
            rows = slice(h * HD, (h + 1) * HD)
            fresh = exact(vbuf[2 + f, rows, :], kbuf[rows, :], NT)
            state = decay(f, h) * scur[h, 0:HD, :] + fresh
            scur[h, 0:HD, :] = state
            sloc[f, h] = state

        @pl.when(f == 2)
        def _():
            y_ring(0).wait_recv()
            y_ring(1).wait_recv()
            y_ring(2).start()
            y_ring(3).start()

        return 0

    lax.fori_loop(0, FR, key, 0)

    row_id = lax.broadcasted_iota(jnp.int32, (TT, HD), 0)
    half_rows = pl.ds(pl.multiple_of(core * HALF, HALF), HALF)
    other_rows = pl.ds(pl.multiple_of((1 - core) * HALF, HALF), HALF)

    def put_log(ref, log):
        high = log.astype(BF).astype(F32)
        low = log - high
        ref[...] = jnp.where(row_id == 0, high, jnp.where(row_id == 1, low, 0.0)).astype(BF)

    def get_log(ref):
        return jnp.sum(ref[...].astype(F32), axis=0, keepdims=True)

    def flag(condition):
        return jnp.where(condition, 1.0, 0.0).astype(F32)

    def join(early, late):
        return early[0] + late[0], jnp.exp(late[0]) * early[1] + late[1]

    def choose(on, pair, other):
        return tuple(on * a + (1.0 - on) * b for a, b in zip(pair, other))

    def masked(on, pair):
        return tuple(on * a for a in pair)

    def own_log(h):
        log = jnp.full((1, HD), decay_ref[0, h], F32)
        for f in range(1, FR):
            log = log + jnp.full((1, HD), decay_ref[f, h], F32)
        return log

    first_core = flag(core == 0)

    def chip_pair(h):
        own = own_log(h), scur[h, half_rows, :]
        other = get_log(full_in.at[h, 128:144]), full_in[h, half_rows, :].astype(F32)
        return join(choose(first_core, own, other), choose(first_core, other, own))

    def put(slot, h, pair):
        half_out[slot, h, 0:HALF, :] = pair[1].astype(BF)
        put_log(half_out.at[slot, h, HALF : HALF + TT], pair[0])

    def get(slot, h):
        return (
            get_log(half_in.at[slot, h, HALF : HALF + TT]),
            half_in[slot, h, 0:HALF, :].astype(F32),
        )

    def scan_core():
        return remote(SCAN, full_out, full_in, twin)

    def scan_y(step):
        return remote(SCAN + step, half_out.at[0], half_in.at[step - 1], y_peer(step))

    def scan_z(step):
        return remote(SCAN + 3 + step, half_out.at[1], half_in.at[2 + step], z_peer(step))

    def scan_end():
        return remote(SCAN + 7, end_out, end_in, twin)

    def prefix(place, slot, h):
        total = None
        for step in (3, 2, 1):
            pair = masked(flag(place >= step), get(slot + step, h))
            total = pair if total is None else join(total, pair)
        return total

    for h in range(NH):
        full_out[h, 0:128, :] = scur[h].astype(BF)
        put_log(full_out.at[h, 128:144], own_log(h))
    scan_core().start()

    def frame_of(p):
        return (sp + 4 - RELS[p]) % 4

    load_wq.wait()

    def query(p):
        project(2, frame_of(p), qbuf.at[frame_of(p)])

    query(1)

    scan_core().wait_recv()
    for h in range(NH):
        put(0, h, chip_pair(h))
    for step in (1, 2, 3):
        scan_y(step).start()

    query(2)
    mixed_t = exact(spots(TT, TT, lambda r: r, lambda l: l), mix_ref[...], NT).astype(BF)
    mine = exact(
        spots(8, 128, lambda r: r + FR * tm, lambda l: l), list_ref[...].astype(BF), NT
    )
    mine = (mine - (FR * tm - WIN).astype(F32)).astype(BF)
    for n in range(NBR):
        mixrep[n] = exact(
            mixed_t, spots(128, 128, lambda r: r, lambda l: l % TT + n * TT)
        )
        listed = exact(
            mine, spots(TILES * NBR, ROWS, lambda r: r, lambda l: l // TT * NBR + n)
        )
        for f in range(FR):
            rel[f, n : n + 1, :] = listed[f : f + 1]

    query(3)

    for step in (1, 2, 3):
        scan_y(step).wait_recv()
    for h in range(NH):
        total = join(prefix(y, -1, h), chip_pair(h))
        for step in (3, 2, 1):
            total = join(total, masked(flag(y < step), get(step - 1, h)))
        put(1, h, total)
    for step in (1, 2, 3):
        scan_z(step).start()

    halo_left().wait_recv()
    halo_right().wait_recv()
    tile_of_lane = lax.broadcasted_iota(jnp.int32, (TT, 128), 1) // TT

    def window(p):
        f = frame_of(p)

        def tiles(j, _):
            cols = pl.ds(pl.multiple_of(j * 128, 128), 128)
            for g in range(2 * WIN + 1):
                block = jnp.zeros((TT, 128), F32)
                for n in range(NBR):
                    listed = rel[f, n : n + 1, cols]
                    block = block + jnp.where(listed == (f + g).astype(F32), mixrep[n], 0.0)
                for t in range(8):
                    low = g * 128 + t * TT
                    band[low : low + TT, :] = jnp.where(tile_of_lane == t, block, 0.0).astype(BF)
            source = jnp.concatenate([vbuf[f + g, :, cols] for g in range(2 * WIN + 1)], axis=1)
            win[f, :, cols] = exact(source, band[...]).astype(BF)
            return 0

        lax.fori_loop(0, ROWS // 128, tiles, 0)

    window(1)
    window(2)

    for step in (1, 2, 3):
        scan_z(step).wait_recv()
    for h in range(NH):
        half = join(prefix(z, 2, h), prefix(y, -1, h))[1]
        entry[h, half_rows, :] = half
        end_out[h] = half.astype(BF)
    scan_end().start()

    for p in (2, 3):
        z_pass(p, 0).wait_recv()
        z_pass(p, 1).wait_recv()
        to_twin(p).start()
    y_ring(2).wait_recv()
    y_ring(3).wait_recv()
    to_twin(1).start()

    window(3)

    scan_end().wait_recv()
    for h in range(NH):
        entry[h, other_rows, :] = end_in[h].astype(F32)
        before = get_log(full_in.at[h, 128:144]), full_in[h, 0:HD, :].astype(F32)
        before = masked(1.0 - first_core, before)
        entering = jnp.exp(before[0]) * entry[h, 0:HD, :] + before[1]
        for f in range(FR):
            entering = decay(f, h) * entering
            sloc[f, h] = sloc[f, h] + entering

    def swap(p):
        return remote(
            SWAP + p - 1,
            qbuf.at[frame_of(p)],
            mixb.at[pl.ds(p * GP, GW)],
            x_peer(4 - RELS[p]),
        )

    def attend(p):
        f = frame_of(p)
        for h in range(NH):
            rows = slice(h * HD, (h + 1) * HD)
            state = jnp.zeros((HD, HD), F32)
            for g in range(FR):
                state = state + flag(last_ref[f] == FR * tm + g) * sloc[g, h]
            linear = exact(state.astype(BF), qbuf[f, rows, :])
            inverse = lax.rsqrt(
                jnp.sum(linear * linear, axis=0, keepdims=True) * (1.0 / HD) + EPS
            )
            both = (linear * inverse + win[f, rows, :].astype(F32)).astype(BF)
            if p == 0:
                mixb[rows, :] = both
            else:
                qbuf[f, rows, :] = both

    for p in (1, 2, 3):
        attend(p)
        swap(p).start()
    query(0)
    window(0)
    attend(0)

    load_resid.wait()

    def weights(i, p, count):
        return wo[i, :, :, p * GP : (p + count) * GP].reshape(2 * PART, count * GP)

    for i in range(4):
        low, high = i * 2 * PART, min((i + 1) * 2 * PART, D)
        acc[low:high, :] = exact(weights(i, 0, 1)[: high - low], mixb[0:GP, :])

    to_twin(1).wait_recv()
    swap(1).wait_recv()
    for i in range(4):
        low, high = i * 2 * PART, min((i + 1) * 2 * PART, D)
        acc[low:high, :] += exact(weights(i, 1, 1)[: high - low], mixb[GP : 2 * GP, :])

    def store(i):
        rows = pl.ds(i * 2 * PART, min(2 * PART, D - i * 2 * PART))
        return load(9 + i, resid.at[rows], out_hbm.at[rows])

    for p in (2, 3):
        to_twin(p).wait_recv()
        swap(p).wait_recv()
    for i in range(4):
        low, high = i * 2 * PART, min((i + 1) * 2 * PART, D)
        total = acc[low:high, :] + exact(weights(i, 2, 2)[: high - low], mixb[2 * GP : 4 * GP, :])
        for c in range(ROWS // 128):
            cols = slice(c * 128, (c + 1) * 128)
            resid[low:high, cols] = (
                resid[low:high, cols].astype(F32) + gains[low:high, 256:384] * total[:, cols]
            ).astype(BF)
        store(i).start()

    for p in (1, 2, 3):
        x_gather(p).wait_send()
        to_twin(p).wait_send()
        swap(p).wait_send()
        scan_y(p).wait_send()
        scan_z(p).wait_send()
    for p in (2, 3):
        x_gather(p, 1).wait_send()
        z_pass(p, 0).wait_send()
        z_pass(p, 1).wait_send()
    for k in range(4):
        y_ring(k).wait_send()
    scan_core().wait_send()
    scan_end().wait_send()
    halo_left().wait_send()
    halo_right().wait_send()
    for i in range(4):
        store(i).wait()


def body(
    tokens, mod_scale, mod_shift, out_gate, w_query, w_key, w_value, w_out,
    log_decay, mix_weight, block_last, win_list,
):
    anywhere = pl.BlockSpec(memory_space=pl.ANY)
    vmem = pl.BlockSpec(memory_space=pltpu.VMEM)
    smem = pl.BlockSpec(memory_space=pltpu.SMEM)
    out = pl.pallas_call(
        kernel,
        out_shape=jax.ShapeDtypeStruct((D, ROWS), BF),
        in_specs=[anywhere, vmem, vmem, vmem] + [anywhere] * 4 + [vmem, smem, smem, vmem],
        out_specs=anywhere,
        scratch_shapes=[
            pltpu.VMEM((FR, D, ROWS), BF),
            pltpu.VMEM((D, ROWS), BF),
            pltpu.VMEM((3, GW, D), BF),
            pltpu.VMEM((GP, D), BF),
            pltpu.VMEM((4, 2, PART, 4 * GP), BF),
            pltpu.VMEM((2 * FR, GW, ROWS), BF),
            pltpu.VMEM((GW, ROWS), BF),
            pltpu.VMEM((FR, GW, ROWS), BF),
            pltpu.VMEM((FR, GW, ROWS), BF),
            pltpu.VMEM((4 * GP, ROWS), BF),
            pltpu.VMEM((D, ROWS), F32),
            pltpu.VMEM((D, 384), F32),
            pltpu.VMEM((FR, NH, HD, HD), F32),
            pltpu.VMEM((NH, 128, HD), F32),
            pltpu.VMEM((NH, 128, HD), F32),
            pltpu.VMEM((NH, 144, HD), BF),
            pltpu.VMEM((NH, 144, HD), BF),
            pltpu.VMEM((2, NH, HALF + TT, HD), BF),
            pltpu.VMEM((6, NH, HALF + TT, HD), BF),
            pltpu.VMEM((NH, HALF, HD), BF),
            pltpu.VMEM((NH, HALF, HD), BF),
            pltpu.VMEM((NBR, TT, 128), F32),
            pltpu.VMEM((FR, NBR, ROWS), F32),
            pltpu.VMEM(((2 * WIN + 1) * 128, 128), BF),
            pltpu.SemaphoreType.DMA((13,)),
            pltpu.SemaphoreType.DMA((MESSAGES,)),
            pltpu.SemaphoreType.DMA((MESSAGES,)),
        ],
        compiler_params=pltpu.CompilerParams(
            collective_id=0, has_side_effects=True, vmem_limit_bytes=66_000_000
        ),
    )(
        tokens.T,
        mod_scale,
        mod_shift,
        out_gate,
        w_query.T,
        w_key.T,
        w_value.T,
        w_out,
        mix_weight.reshape(NBR * TT, TT),
        log_decay,
        block_last,
        win_list.transpose(1, 2, 0).reshape(TILES * NBR, -1),
    )
    return out.T


def solution(mesh):
    placed = (
        P("tm", None),
        P(),
        P(),
        P(),
        P(None, "space"),
        P(None, "space"),
        P(None, "space"),
        P("space", None),
        P("tm", "space"),
        P(),
        P("tm"),
        P(),
    )
    return jax.shard_map(
        body, mesh=mesh, in_specs=placed, out_specs=P(("tm", "space"), None), check_vma=False
    )
```

```python
import jax
import jax.numpy as jnp
from jax import lax
from jax.experimental import pallas as pl
from jax.experimental.pallas import tpu as pltpu
from jax.sharding import PartitionSpec as P

HD = 112
NH = 5
GW = NH * HD
GP = 640
D = 2240
FR = 4
ROWS = 512
TILES = 32
TT = 16
NBR = 8
WIN = 2
PART = 288
EPS = 1e-06
RELS = (0, 2, 3, 1)
MESH = pl.DeviceIdType.MESH
BF = jnp.bfloat16
F32 = jnp.float32
NT = (((1,), (1,)), ((), ()))

X_GATHER = 0
FORWARD = 4
Z_PASS = 6
TWIN = 12
HALO = 15
SCAN = 17
SWAP = 25
MESSAGES = 29
HALF = 64


def kernel(
    tok_hbm, scale_ref, shift_ref, gate_ref, wq_hbm, wk_hbm, wv_hbm, wo_hbm, mix_ref,
    decay_ref, last_ref, list_ref, out_hbm,
    tok, resid, wqkv, wo_raw, wo, vbuf, kbuf, qbuf, win, mixb, acc, gains,
    relay, sloc, scur, entry, full_out, full_in, half_out, half_in, end_out, end_in,
    mixrep, rel, band, local_sem, send_sem, recv_sem,
):
    tm = lax.axis_index("tm")
    sp = lax.axis_index("space")
    z, y, core = tm // 8, (tm // 2) % 4, tm % 2

    def at(zz, yy, cc):
        return (zz * 8 + yy * 2 + cc, sp)

    def x_peer(step):
        return (tm, (sp + step) % 4)

    def z_peer(step):
        return at((z + step) % 4, y, core)

    def y_peer(step):
        return at(z, (y + step) % 4, core)

    twin = at(z, y, 1 - core)
    right = ((tm + 1) % 32, sp)
    left = ((tm + 31) % 32, sp)
    outer = ((tm + 31 + 2 * core) % 32, sp)

    def remote(number, src, dst, device):
        return pltpu.make_async_remote_copy(
            src_ref=src,
            dst_ref=dst,
            send_sem=send_sem.at[number],
            recv_sem=recv_sem.at[number],
            device_id=device,
            device_id_type=MESH,
        )

    def load(number, src, dst):
        return pltpu.make_async_copy(src, dst, local_sem.at[number])

    load_wo = load(0, wo_hbm, wo_raw.at[pl.ds(0, GW)])
    load_wv = load(1, wv_hbm, wqkv.at[0])
    load_wk = load(2, wk_hbm, wqkv.at[1])
    load_wq = load(3, wq_hbm, wqkv.at[2])
    own_rows = pl.ds(pl.multiple_of(sp * ROWS, ROWS), ROWS)
    load_resid = load(4, tok_hbm.at[:, own_rows], resid)

    def load_tok(f):
        rows = pl.ds(pl.multiple_of(f * ROWS, ROWS), ROWS)
        return load(5 + f, tok_hbm.at[:, rows], tok.at[f])

    load_wo.start()
    load_tok(0).start()
    load_wv.start()
    for f in range(1, FR):
        load_tok(f).start()
    load_wk.start()
    load_wq.start()
    load_resid.start()

    barrier = pltpu.get_barrier_semaphore()
    partners = [x_peer(i) for i in (1, 3)] + [y_peer(i) for i in (1, 2, 3)]
    partners += [z_peer(i) for i in (1, 2, 3)] + [twin, outer]
    for device in partners:
        pl.semaphore_signal(barrier, inc=1, device_id=device, device_id_type=MESH)

    def spots(rows, lanes, of_row, of_lane):
        r = lax.broadcasted_iota(jnp.int32, (rows, lanes), 0)
        l = lax.broadcasted_iota(jnp.int32, (rows, lanes), 1)
        return jnp.where(of_row(r) == of_lane(l), 1.0, 0.0).astype(BF)

    def exact(a, b, dims=(((1,), (0,)), ((), ()))):
        return lax.dot_general(a, b, dims, preferred_element_type=F32)

    for p in range(4):
        mixb[p * GP + GW : (p + 1) * GP, :] = jnp.zeros((GP - GW, ROWS), BF)

    wo_raw[GW:GP, :] = jnp.zeros((GP - GW, D), BF)
    wo[3, 1, D - 7 * PART : PART, 0:GP] = jnp.zeros((8 * PART - D, GP), BF)
    load_wo.wait()
    for low in range(0, D, 256):
        high = min(low + 256, D)
        eye = spots(high - low, high - low, lambda r: r, lambda l: l)
        turned = exact(eye, wo_raw[:, low:high], NT).astype(BF)
        for part in range(8):
            first, last = max(low, part * PART), min(high, (part + 1) * PART)
            if first < last:
                wo[part // 2, part % 2, first - part * PART : last - part * PART, 0:GP] = turned[
                    first - low : last - low
                ]

    pl.semaphore_wait(barrier, len(partners))

    def chunk(p, i):
        return wo.at[i, core, :, pl.ds(p * GP, GP)]

    onward = x_peer(1 + 2 * core)

    def x_gather(p, second):
        i = (z + second) % 4
        number = X_GATHER + (p - 2) * 2 + second
        return remote(number, chunk(0, i), chunk(p, i), x_peer(4 - RELS[p]))

    def x_forward(second):
        i = (z + second) % 4
        cols = pl.ds(pl.multiple_of((2 + core) * GP, 128), GP)
        return remote(FORWARD + second, wo.at[i, core, :, cols], chunk(1, i), onward)

    def z_pass(p, second):
        ref = chunk(p, (z + second) % 4)
        return remote(Z_PASS + (p - 1) * 2 + second, ref, ref, z_peer(3 if second else 1))

    def x_arrived(second):
        for p in (2, 3):
            x_gather(p, second).wait_recv()
            z_pass(p, second).start()
        x_forward(second).start()

    def to_twin(p):
        ref = wo.at[:, core, :, pl.ds(p * GP, GP)]
        return remote(TWIN + p - 1, ref, ref, twin)

    for second in (0, 1):
        for p in (2, 3):
            x_gather(p, second).start()

    parts = []
    for vector in (1.0 + scale_ref[...], shift_ref[...], gate_ref[...]):
        rest = vector.reshape(1, D)
        for _ in range(3):
            part = rest.astype(BF)
            parts.append(part)
            rest = rest - part.astype(F32)
    parts = jnp.concatenate(parts + [jnp.zeros((7, D), BF)], axis=0)
    gains[...] = exact(
        parts, spots(16, 384, lambda r: r // 3, lambda l: l // 128), (((0,), (0,)), ((), ()))
    )

    def norm(f):
        rows = 32

        def squares(i, total):
            x = tok[f, pl.ds(pl.multiple_of(i * rows, rows), rows), :].astype(F32)
            return total + jnp.sum((x * x).reshape(rows // 8, 8, ROWS), axis=0)

        total = lax.fori_loop(0, D // rows, squares, jnp.zeros((8, ROWS), F32), unroll=2)
        inverse = lax.rsqrt(jnp.sum(total, axis=0, keepdims=True) * (1.0 / D) + EPS)

        def scale(i, _):
            r = pl.ds(pl.multiple_of(i * rows, rows), rows)
            gain, shift = gains[r, 0:128], gains[r, 128:256]
            for c in range(ROWS // 128):
                cols = slice(c * 128, (c + 1) * 128)
                x = tok[f, r, cols].astype(F32)
                tok[f, r, cols] = (x * inverse[:, cols] * gain + shift).astype(BF)
            return 0

        lax.fori_loop(0, D // rows, scale, 0, unroll=2)

    def halo_left():
        return remote(HALO, vbuf.at[pl.ds(2, 2)], vbuf.at[pl.ds(6, 2)], left)

    def halo_right():
        return remote(HALO + 1, vbuf.at[pl.ds(4, 2)], vbuf.at[pl.ds(0, 2)], right)

    def decay(f, h):
        return jnp.exp(jnp.full((1, HD), decay_ref[f, h], F32))

    def project(weight, f, dst):
        for half in range(2):
            cols = slice(half * 256, (half + 1) * 256)
            dst[:, cols] = jnp.dot(
                wqkv[weight], tok[f, :, cols], preferred_element_type=F32
            ).astype(BF)

    load_wv.wait()

    def value(f, _):
        load_tok(f).wait()
        norm(f)
        project(0, f, vbuf.at[2 + f])

        @pl.when(f == 1)
        def _():
            halo_left().start()

        @pl.when(f == 2)
        def _():
            x_arrived(0)

        @pl.when(f == 3)
        def _():
            halo_right().start()

        return 0

    lax.fori_loop(0, FR, value, 0)

    load_wk.wait()
    scur[...] = jnp.zeros_like(scur)

    def key(f, _):
        project(1, f, kbuf)
        for h in range(NH):
            rows = slice(h * HD, (h + 1) * HD)
            fresh = exact(vbuf[2 + f, rows, :], kbuf[rows, :], NT)
            state = decay(f, h) * scur[h, 0:HD, :] + fresh
            scur[h, 0:HD, :] = state
            sloc[f, h] = state

        @pl.when(f == 1)
        def _():
            x_arrived(1)

        return 0

    lax.fori_loop(0, FR, key, 0)

    row_id = lax.broadcasted_iota(jnp.int32, (TT, HD), 0)
    half_rows = pl.ds(pl.multiple_of(core * HALF, HALF), HALF)
    other_rows = pl.ds(pl.multiple_of((1 - core) * HALF, HALF), HALF)

    def put_log(ref, log):
        high = log.astype(BF).astype(F32)
        low = log - high
        ref[...] = jnp.where(row_id == 0, high, jnp.where(row_id == 1, low, 0.0)).astype(BF)

    def get_log(ref):
        return jnp.sum(ref[...].astype(F32), axis=0, keepdims=True)

    def flag(condition):
        return jnp.where(condition, 1.0, 0.0).astype(F32)

    def join(early, late):
        return early[0] + late[0], jnp.exp(late[0]) * early[1] + late[1]

    def choose(on, pair, other):
        return tuple(on * a + (1.0 - on) * b for a, b in zip(pair, other))

    def masked(on, pair):
        return tuple(on * a for a in pair)

    def own_log(h):
        log = jnp.full((1, HD), decay_ref[0, h], F32)
        for f in range(1, FR):
            log = log + jnp.full((1, HD), decay_ref[f, h], F32)
        return log

    first_core = flag(core == 0)

    def chip_pair(h):
        own = own_log(h), scur[h, half_rows, :]
        other = get_log(full_in.at[h, 128:144]), full_in[h, half_rows, :].astype(F32)
        return join(choose(first_core, own, other), choose(first_core, other, own))

    def put(slot, h, pair):
        half_out[slot, h, 0:HALF, :] = pair[1].astype(BF)
        put_log(half_out.at[slot, h, HALF : HALF + TT], pair[0])

    def get(slot, h):
        return (
            get_log(half_in.at[slot, h, HALF : HALF + TT]),
            half_in[slot, h, 0:HALF, :].astype(F32),
        )

    def scan_core():
        return remote(SCAN, full_out, full_in, twin)

    def scan_y(step):
        return remote(SCAN + step, half_out.at[0], half_in.at[step - 1], y_peer(step))

    def scan_z(step):
        return remote(SCAN + 3 + step, half_out.at[1], half_in.at[2 + step], z_peer(step))

    def scan_end():
        return remote(SCAN + 7, end_out, end_in, twin)

    def prefix(place, slot, h):
        total = None
        for step in (3, 2, 1):
            pair = masked(flag(place >= step), get(slot + step, h))
            total = pair if total is None else join(total, pair)
        return total

    for h in range(NH):
        full_out[h, 0:128, :] = scur[h].astype(BF)
        put_log(full_out.at[h, 128:144], own_log(h))
    scan_core().start()

    def frame_of(p):
        return (sp + 4 - RELS[p]) % 4

    load_wq.wait()

    def query(p):
        project(2, frame_of(p), qbuf.at[frame_of(p)])

    query(1)

    scan_core().wait_recv()
    for h in range(NH):
        put(0, h, chip_pair(h))
    for step in (1, 2, 3):
        scan_y(step).start()

    query(2)
    mixed_t = exact(spots(TT, TT, lambda r: r, lambda l: l), mix_ref[...], NT).astype(BF)
    mine = exact(
        spots(8, 128, lambda r: r + FR * tm, lambda l: l), list_ref[...].astype(BF), NT
    )
    mine = (mine - (FR * tm - WIN).astype(F32)).astype(BF)
    for n in range(NBR):
        mixrep[n] = exact(
            mixed_t, spots(128, 128, lambda r: r, lambda l: l % TT + n * TT)
        )
        listed = exact(
            mine, spots(TILES * NBR, ROWS, lambda r: r, lambda l: l // TT * NBR + n)
        )
        for f in range(FR):
            rel[f, n : n + 1, :] = listed[f : f + 1]

    query(3)

    for step in (1, 2, 3):
        scan_y(step).wait_recv()
    for h in range(NH):
        total = join(prefix(y, -1, h), chip_pair(h))
        for step in (3, 2, 1):
            total = join(total, masked(flag(y < step), get(step - 1, h)))
        put(1, h, total)
    for step in (1, 2, 3):
        scan_z(step).start()

    halo_left().wait_recv()
    halo_right().wait_recv()
    tile_of_lane = lax.broadcasted_iota(jnp.int32, (TT, 128), 1) // TT

    def window(p):
        f = frame_of(p)

        def tiles(j, _):
            cols = pl.ds(pl.multiple_of(j * 128, 128), 128)
            for g in range(2 * WIN + 1):
                block = jnp.zeros((TT, 128), F32)
                for n in range(NBR):
                    listed = rel[f, n : n + 1, cols]
                    block = block + jnp.where(listed == (f + g).astype(F32), mixrep[n], 0.0)
                for t in range(8):
                    low = g * 128 + t * TT
                    band[low : low + TT, :] = jnp.where(tile_of_lane == t, block, 0.0).astype(BF)
            source = jnp.concatenate([vbuf[f + g, :, cols] for g in range(2 * WIN + 1)], axis=1)
            win[f, :, cols] = exact(source, band[...]).astype(BF)
            return 0

        lax.fori_loop(0, ROWS // 128, tiles, 0)

    window(1)
    window(2)

    for step in (1, 2, 3):
        scan_z(step).wait_recv()
    for h in range(NH):
        half = join(prefix(z, 2, h), prefix(y, -1, h))[1]
        entry[h, half_rows, :] = half
        end_out[h] = half.astype(BF)
    scan_end().start()

    for second in (0, 1):
        x_forward(second).wait_recv()
        z_pass(1, second).start()
    for p in (2, 3):
        z_pass(p, 0).wait_recv()
        z_pass(p, 1).wait_recv()
        to_twin(p).start()

    window(3)

    scan_end().wait_recv()
    for h in range(NH):
        entry[h, other_rows, :] = end_in[h].astype(F32)
        before = get_log(full_in.at[h, 128:144]), full_in[h, 0:HD, :].astype(F32)
        before = masked(1.0 - first_core, before)
        entering = jnp.exp(before[0]) * entry[h, 0:HD, :] + before[1]
        for f in range(FR):
            entering = decay(f, h) * entering
            sloc[f, h] = sloc[f, h] + entering

    def swap(p):
        mixed = qbuf.at[frame_of(p)]
        if p == 1:
            return remote(SWAP + 2, mixed, relay, onward)
        return remote(SWAP + p - 2, mixed, mixb.at[pl.ds(p * GP, GW)], x_peer(4 - RELS[p]))

    def swap_onward():
        return remote(SWAP + 3, relay, mixb.at[pl.ds(GP, GW)], onward)

    def attend(p):
        f = frame_of(p)
        for h in range(NH):
            rows = slice(h * HD, (h + 1) * HD)
            state = jnp.zeros((HD, HD), F32)
            for g in range(FR):
                state = state + flag(last_ref[f] == FR * tm + g) * sloc[g, h]
            linear = exact(state.astype(BF), qbuf[f, rows, :])
            inverse = lax.rsqrt(
                jnp.sum(linear * linear, axis=0, keepdims=True) * (1.0 / HD) + EPS
            )
            both = (linear * inverse + win[f, rows, :].astype(F32)).astype(BF)
            if p == 0:
                mixb[rows, :] = both
            else:
                qbuf[f, rows, :] = both

    for p in (1, 2, 3):
        attend(p)
        swap(p).start()
    query(0)
    window(0)
    attend(0)
    swap(1).wait_recv()
    swap_onward().start()
    z_pass(1, 0).wait_recv()
    z_pass(1, 1).wait_recv()
    to_twin(1).start()

    load_resid.wait()

    def weights(i, p, count):
        return wo[i, :, :, p * GP : (p + count) * GP].reshape(2 * PART, count * GP)

    for i in range(4):
        low, high = i * 2 * PART, min((i + 1) * 2 * PART, D)
        acc[low:high, :] = exact(weights(i, 0, 1)[: high - low], mixb[0:GP, :])

    for p in (2, 3):
        to_twin(p).wait_recv()
        swap(p).wait_recv()
    for i in range(4):
        low, high = i * 2 * PART, min((i + 1) * 2 * PART, D)
        acc[low:high, :] += exact(weights(i, 2, 2)[: high - low], mixb[2 * GP : 4 * GP, :])

    def store(i):
        rows = pl.ds(i * 2 * PART, min(2 * PART, D - i * 2 * PART))
        return load(9 + i, resid.at[rows], out_hbm.at[rows])

    to_twin(1).wait_recv()
    swap_onward().wait_recv()
    for i in range(4):
        low, high = i * 2 * PART, min((i + 1) * 2 * PART, D)
        total = acc[low:high, :] + exact(weights(i, 1, 1)[: high - low], mixb[GP : 2 * GP, :])
        for c in range(ROWS // 128):
            cols = slice(c * 128, (c + 1) * 128)
            resid[low:high, cols] = (
                resid[low:high, cols].astype(F32) + gains[low:high, 256:384] * total[:, cols]
            ).astype(BF)
        store(i).start()

    for p in (1, 2, 3):
        to_twin(p).wait_send()
        swap(p).wait_send()
        scan_y(p).wait_send()
        scan_z(p).wait_send()
    for second in (0, 1):
        for p in (1, 2, 3):
            z_pass(p, second).wait_send()
            if p > 1:
                x_gather(p, second).wait_send()
        x_forward(second).wait_send()
    swap_onward().wait_send()
    scan_core().wait_send()
    scan_end().wait_send()
    halo_left().wait_send()
    halo_right().wait_send()
    for i in range(4):
        store(i).wait()


def body(
    tokens, mod_scale, mod_shift, out_gate, w_query, w_key, w_value, w_out,
    log_decay, mix_weight, block_last, win_list,
):
    anywhere = pl.BlockSpec(memory_space=pl.ANY)
    vmem = pl.BlockSpec(memory_space=pltpu.VMEM)
    smem = pl.BlockSpec(memory_space=pltpu.SMEM)
    out = pl.pallas_call(
        kernel,
        out_shape=jax.ShapeDtypeStruct((D, ROWS), BF),
        in_specs=[anywhere, vmem, vmem, vmem] + [anywhere] * 4 + [vmem, smem, smem, vmem],
        out_specs=anywhere,
        scratch_shapes=[
            pltpu.VMEM((FR, D, ROWS), BF),
            pltpu.VMEM((D, ROWS), BF),
            pltpu.VMEM((3, GW, D), BF),
            pltpu.VMEM((GP, D), BF),
            pltpu.VMEM((4, 2, PART, 4 * GP), BF),
            pltpu.VMEM((2 * FR, GW, ROWS), BF),
            pltpu.VMEM((GW, ROWS), BF),
            pltpu.VMEM((FR, GW, ROWS), BF),
            pltpu.VMEM((FR, GW, ROWS), BF),
            pltpu.VMEM((4 * GP, ROWS), BF),
            pltpu.VMEM((D, ROWS), F32),
            pltpu.VMEM((D, 384), F32),
            pltpu.VMEM((GW, ROWS), BF),
            pltpu.VMEM((FR, NH, HD, HD), F32),
            pltpu.VMEM((NH, 128, HD), F32),
            pltpu.VMEM((NH, 128, HD), F32),
            pltpu.VMEM((NH, 144, HD), BF),
            pltpu.VMEM((NH, 144, HD), BF),
            pltpu.VMEM((2, NH, HALF + TT, HD), BF),
            pltpu.VMEM((6, NH, HALF + TT, HD), BF),
            pltpu.VMEM((NH, HALF, HD), BF),
            pltpu.VMEM((NH, HALF, HD), BF),
            pltpu.VMEM((NBR, TT, 128), F32),
            pltpu.VMEM((FR, NBR, ROWS), F32),
            pltpu.VMEM(((2 * WIN + 1) * 128, 128), BF),
            pltpu.SemaphoreType.DMA((13,)),
            pltpu.SemaphoreType.DMA((MESSAGES,)),
            pltpu.SemaphoreType.DMA((MESSAGES,)),
        ],
        compiler_params=pltpu.CompilerParams(
            collective_id=0, has_side_effects=True, vmem_limit_bytes=66_000_000
        ),
    )(
        tokens.T,
        mod_scale,
        mod_shift,
        out_gate,
        w_query.T,
        w_key.T,
        w_value.T,
        w_out,
        mix_weight.reshape(NBR * TT, TT),
        log_decay,
        block_last,
        win_list.transpose(1, 2, 0).reshape(TILES * NBR, -1),
    )
    return out.T


def solution(mesh):
    placed = (
        P("tm", None),
        P(),
        P(),
        P(),
        P(None, "space"),
        P(None, "space"),
        P(None, "space"),
        P("space", None),
        P("tm", "space"),
        P(),
        P("tm"),
        P(),
    )
    return jax.shard_map(
        body, mesh=mesh, in_specs=placed, out_specs=P(("tm", "space"), None), check_vma=False
    )
```

```python
import jax
import jax.numpy as jnp
from jax import lax
from jax.experimental import pallas as pl
from jax.experimental.pallas import tpu as pltpu
from jax.sharding import PartitionSpec as P

HD = 112
NH = 5
GW = NH * HD
GP = 640
D = 2240
FR = 4
ROWS = 512
TILES = 32
TT = 16
NBR = 8
WIN = 2
PART = 288
EPS = 1e-06
RELS = (0, 2, 3, 1)
MESH = pl.DeviceIdType.MESH
BF = jnp.bfloat16
F32 = jnp.float32
NT = (((1,), (1,)), ((), ()))

X_GATHER = 0
FORWARD = 4
SIDE_PASS = 6
TWIN = 12
HALO = 15
SCAN = 17
SWAP = 25
MESSAGES = 29
HALF = 64


def kernel(
    tok_hbm, scale_ref, shift_ref, gate_ref, wq_hbm, wk_hbm, wv_hbm, wo_hbm, mix_ref,
    decay_ref, last_ref, list_ref, out_hbm,
    tok, resid, wqkv, wo_raw, wo, vbuf, kbuf, qbuf, win, mixb, acc, gains,
    relay, sloc, scur, entry, full_out, full_in, half_out, half_in, end_out, end_in,
    mixrep, rel, band, local_sem, send_sem, recv_sem,
):
    tm = lax.axis_index("tm")
    sp = lax.axis_index("space")
    z, y, core = tm // 8, (tm // 2) % 4, tm % 2

    def at(zz, yy, cc):
        return (zz * 8 + yy * 2 + cc, sp)

    def x_peer(step):
        return (tm, (sp + step) % 4)

    def z_peer(step):
        return at((z + step) % 4, y, core)

    def y_peer(step):
        return at(z, (y + step) % 4, core)

    twin = at(z, y, 1 - core)
    right = ((tm + 1) % 32, sp)
    left = ((tm + 31) % 32, sp)
    outer = ((tm + 31 + 2 * core) % 32, sp)

    def remote(number, src, dst, device):
        return pltpu.make_async_remote_copy(
            src_ref=src,
            dst_ref=dst,
            send_sem=send_sem.at[number],
            recv_sem=recv_sem.at[number],
            device_id=device,
            device_id_type=MESH,
        )

    def load(number, src, dst):
        return pltpu.make_async_copy(src, dst, local_sem.at[number])

    load_wo = load(0, wo_hbm, wo_raw.at[pl.ds(0, GW)])
    load_wv = load(1, wv_hbm, wqkv.at[0])
    load_wk = load(2, wk_hbm, wqkv.at[1])
    load_wq = load(3, wq_hbm, wqkv.at[2])
    own_rows = pl.ds(pl.multiple_of(sp * ROWS, ROWS), ROWS)
    load_resid = load(4, tok_hbm.at[:, own_rows], resid)

    def load_tok(f):
        rows = pl.ds(pl.multiple_of(f * ROWS, ROWS), ROWS)
        return load(5 + f, tok_hbm.at[:, rows], tok.at[f])

    load_wo.start()
    load_tok(0).start()
    load_wv.start()
    for f in range(1, FR):
        load_tok(f).start()
    load_wk.start()
    load_wq.start()
    load_resid.start()

    barrier = pltpu.get_barrier_semaphore()
    partners = [x_peer(i) for i in (1, 3)] + [y_peer(i) for i in (1, 2, 3)]
    partners += [z_peer(i) for i in (1, 2, 3)] + [twin, outer]
    for device in partners:
        pl.semaphore_signal(barrier, inc=1, device_id=device, device_id_type=MESH)

    def spots(rows, lanes, of_row, of_lane):
        r = lax.broadcasted_iota(jnp.int32, (rows, lanes), 0)
        l = lax.broadcasted_iota(jnp.int32, (rows, lanes), 1)
        return jnp.where(of_row(r) == of_lane(l), 1.0, 0.0).astype(BF)

    def exact(a, b, dims=(((1,), (0,)), ((), ()))):
        return lax.dot_general(a, b, dims, preferred_element_type=F32)

    for p in range(4):
        mixb[p * GP + GW : (p + 1) * GP, :] = jnp.zeros((GP - GW, ROWS), BF)

    wo_raw[GW:GP, :] = jnp.zeros((GP - GW, D), BF)
    wo[3, 1, D - 7 * PART : PART, 0:GP] = jnp.zeros((8 * PART - D, GP), BF)
    load_wo.wait()
    for low in range(0, D, 256):
        high = min(low + 256, D)
        eye = spots(high - low, high - low, lambda r: r, lambda l: l)
        turned = exact(eye, wo_raw[:, low:high], NT).astype(BF)
        for part in range(8):
            first, last = max(low, part * PART), min(high, (part + 1) * PART)
            if first < last:
                wo[part // 2, part % 2, first - part * PART : last - part * PART, 0:GP] = turned[
                    first - low : last - low
                ]

    pl.semaphore_wait(barrier, len(partners))

    def chunk(p, i):
        return wo.at[i, core, :, pl.ds(p * GP, GP)]

    onward = x_peer(1 + 2 * core)

    def place(p):
        if p == 2:
            return z, z_peer
        if p == 3:
            return y, y_peer
        return z + core * (y - z), lambda step: at(
            (z + (1 - core) * step) % 4, (y + core * step) % 4, core
        )

    def x_gather(p, second):
        i = (place(p)[0] + second) % 4
        number = X_GATHER + (p - 2) * 2 + second
        return remote(number, chunk(0, i), chunk(p, i), x_peer(4 - RELS[p]))

    def x_forward(second):
        i = (place(1)[0] + second) % 4
        cols = pl.ds(pl.multiple_of((2 + core) * GP, 128), GP)
        return remote(FORWARD + second, wo.at[i, core, :, cols], chunk(1, i), onward)

    def side_pass(p, second):
        i, peer = place(p)
        ref = chunk(p, (i + second) % 4)
        return remote(SIDE_PASS + (p - 1) * 2 + second, ref, ref, peer(3 if second else 1))

    def x_arrived(second):
        for p in (2, 3):
            x_gather(p, second).wait_recv()
            side_pass(p, second).start()
        x_forward(second).start()

    def to_twin(p):
        ref = wo.at[:, core, :, pl.ds(p * GP, GP)]
        return remote(TWIN + p - 1, ref, ref, twin)

    for second in (0, 1):
        for p in (2, 3):
            x_gather(p, second).start()

    parts = []
    for vector in (1.0 + scale_ref[...], shift_ref[...], gate_ref[...]):
        rest = vector.reshape(1, D)
        for _ in range(3):
            part = rest.astype(BF)
            parts.append(part)
            rest = rest - part.astype(F32)
    parts = jnp.concatenate(parts + [jnp.zeros((7, D), BF)], axis=0)
    gains[...] = exact(
        parts, spots(16, 384, lambda r: r // 3, lambda l: l // 128), (((0,), (0,)), ((), ()))
    )

    def norm(f):
        rows = 32

        def squares(i, total):
            x = tok[f, pl.ds(pl.multiple_of(i * rows, rows), rows), :].astype(F32)
            return total + jnp.sum((x * x).reshape(rows // 8, 8, ROWS), axis=0)

        total = lax.fori_loop(0, D // rows, squares, jnp.zeros((8, ROWS), F32), unroll=2)
        inverse = lax.rsqrt(jnp.sum(total, axis=0, keepdims=True) * (1.0 / D) + EPS)

        def scale(i, _):
            r = pl.ds(pl.multiple_of(i * rows, rows), rows)
            gain, shift = gains[r, 0:128], gains[r, 128:256]
            for c in range(ROWS // 128):
                cols = slice(c * 128, (c + 1) * 128)
                x = tok[f, r, cols].astype(F32)
                tok[f, r, cols] = (x * inverse[:, cols] * gain + shift).astype(BF)
            return 0

        lax.fori_loop(0, D // rows, scale, 0, unroll=2)

    def halo_left():
        return remote(HALO, vbuf.at[pl.ds(2, 2)], vbuf.at[pl.ds(6, 2)], left)

    def halo_right():
        return remote(HALO + 1, vbuf.at[pl.ds(4, 2)], vbuf.at[pl.ds(0, 2)], right)

    def decay(f, h):
        return jnp.exp(jnp.full((1, HD), decay_ref[f, h], F32))

    def project(weight, f, dst):
        for half in range(2):
            cols = slice(half * 256, (half + 1) * 256)
            dst[:, cols] = jnp.dot(
                wqkv[weight], tok[f, :, cols], preferred_element_type=F32
            ).astype(BF)

    @pl.when(tm == 0)
    def _():
        vbuf[0:2] = jnp.zeros((2, GW, ROWS), BF)

    @pl.when(tm == 31)
    def _():
        vbuf[6:8] = jnp.zeros((2, GW, ROWS), BF)

    load_wv.wait()

    def value(f, _):
        load_tok(f).wait()
        norm(f)
        project(0, f, vbuf.at[2 + f])

        @pl.when(f == 1)
        def _():
            @pl.when(tm > 0)
            def _():
                halo_left().start()

        @pl.when(f == 2)
        def _():
            x_arrived(0)

        @pl.when(f == 3)
        def _():
            @pl.when(tm < 31)
            def _():
                halo_right().start()

        return 0

    lax.fori_loop(0, FR, value, 0)

    load_wk.wait()
    scur[...] = jnp.zeros_like(scur)

    def key(f, _):
        project(1, f, kbuf)
        for h in range(NH):
            rows = slice(h * HD, (h + 1) * HD)
            fresh = exact(vbuf[2 + f, rows, :], kbuf[rows, :], NT)
            state = decay(f, h) * scur[h, 0:HD, :] + fresh
            scur[h, 0:HD, :] = state
            sloc[f, h] = state

        @pl.when(f == 1)
        def _():
            x_arrived(1)

        return 0

    lax.fori_loop(0, FR, key, 0)

    row_id = lax.broadcasted_iota(jnp.int32, (TT, HD), 0)
    half_rows = pl.ds(pl.multiple_of(core * HALF, HALF), HALF)
    other_rows = pl.ds(pl.multiple_of((1 - core) * HALF, HALF), HALF)

    def put_log(ref, log):
        high = log.astype(BF).astype(F32)
        low = log - high
        ref[...] = jnp.where(row_id == 0, high, jnp.where(row_id == 1, low, 0.0)).astype(BF)

    def get_log(ref):
        return jnp.sum(ref[...].astype(F32), axis=0, keepdims=True)

    def flag(condition):
        return jnp.where(condition, 1.0, 0.0).astype(F32)

    def join(early, late):
        return early[0] + late[0], jnp.exp(late[0]) * early[1] + late[1]

    def choose(on, pair, other):
        return tuple(on * a + (1.0 - on) * b for a, b in zip(pair, other))

    def masked(on, pair):
        return tuple(on * a for a in pair)

    def own_log(h):
        log = jnp.full((1, HD), decay_ref[0, h], F32)
        for f in range(1, FR):
            log = log + jnp.full((1, HD), decay_ref[f, h], F32)
        return log

    first_core = flag(core == 0)

    def chip_pair(h):
        own = own_log(h), scur[h, half_rows, :]
        other = get_log(full_in.at[h, 128:144]), full_in[h, half_rows, :].astype(F32)
        return join(choose(first_core, own, other), choose(first_core, other, own))

    def put(slot, pairs):
        logs = jnp.zeros((TT, HD), F32)
        for h, (log, state) in enumerate(pairs):
            half_out[slot, h * HALF : (h + 1) * HALF, :] = state.astype(BF)
            high = log.astype(BF).astype(F32)
            logs = jnp.where(row_id == 2 * h, high, logs)
            logs = jnp.where(row_id == 2 * h + 1, log - high, logs)
        half_out[slot, NH * HALF :, :] = logs.astype(BF)

    def get(slot, h):
        logs = half_in[slot, NH * HALF :, :].astype(F32)
        log = jnp.sum(jnp.where(row_id // 2 == h, logs, 0.0), axis=0, keepdims=True)
        return log, half_in[slot, h * HALF : (h + 1) * HALF, :].astype(F32)

    def scan_core():
        return remote(SCAN, full_out, full_in, twin)

    def scan_y(step):
        return remote(SCAN + step, half_out.at[0], half_in.at[step - 1], y_peer(step))

    def scan_z(step):
        return remote(SCAN + 3 + step, half_out.at[1], half_in.at[2 + step], z_peer(step))

    def scan_end():
        return remote(SCAN + 7, end_out, end_in, twin)

    def prefix(place, slot, h):
        total = None
        for step in (3, 2, 1):
            pair = masked(flag(place >= step), get(slot + step, h))
            total = pair if total is None else join(total, pair)
        return total

    for h in range(NH):
        full_out[h, 0:128, :] = scur[h].astype(BF)
        put_log(full_out.at[h, 128:144], own_log(h))
    scan_core().start()

    def frame_of(p):
        return (sp + 4 - RELS[p]) % 4

    load_wq.wait()

    def query(p):
        project(2, frame_of(p), qbuf.at[frame_of(p)])

    query(1)

    scan_core().wait_recv()
    put(0, [chip_pair(h) for h in range(NH)])
    for step in (1, 2, 3):
        scan_y(step).start()

    query(2)
    mixed_t = exact(spots(TT, TT, lambda r: r, lambda l: l), mix_ref[...], NT).astype(BF)
    mine = exact(
        spots(8, 128, lambda r: r + FR * tm, lambda l: l), list_ref[...].astype(BF), NT
    )
    mine = (mine - (FR * tm - WIN).astype(F32)).astype(BF)
    for n in range(NBR):
        mixrep[n] = exact(
            mixed_t, spots(128, 128, lambda r: r, lambda l: l % TT + n * TT)
        )
        listed = exact(
            mine, spots(TILES * NBR, ROWS, lambda r: r, lambda l: l // TT * NBR + n)
        )
        for f in range(FR):
            rel[f, n : n + 1, :] = listed[f : f + 1]

    query(3)
    query(0)

    for step in (1, 2, 3):
        scan_y(step).wait_recv()
    totals = []
    for h in range(NH):
        total = join(prefix(y, -1, h), chip_pair(h))
        for step in (3, 2, 1):
            total = join(total, masked(flag(y < step), get(step - 1, h)))
        totals.append(total)
    put(1, totals)
    for step in (1, 2, 3):
        scan_z(step).start()

    @pl.when(tm < 31)
    def _():
        halo_left().wait_recv()

    @pl.when(tm > 0)
    def _():
        halo_right().wait_recv()

    tile_of_lane = lax.broadcasted_iota(jnp.int32, (TT, 128), 1) // TT

    def window(p):
        f = frame_of(p)

        def tiles(j, _):
            cols = pl.ds(pl.multiple_of(j * 128, 128), 128)
            for g in range(2 * WIN + 1):
                block = jnp.zeros((TT, 128), F32)
                for n in range(NBR):
                    listed = rel[f, n : n + 1, cols]
                    block = block + jnp.where(listed == (f + g).astype(F32), mixrep[n], 0.0)
                for t in range(8):
                    low = g * 128 + t * TT
                    band[low : low + TT, :] = jnp.where(tile_of_lane == t, block, 0.0).astype(BF)
            source = jnp.concatenate([vbuf[f + g, :, cols] for g in range(2 * WIN + 1)], axis=1)
            win[f, :, cols] = exact(source, band[...]).astype(BF)
            return 0

        lax.fori_loop(0, ROWS // 128, tiles, 0)

    window(1)
    window(2)
    window(3)

    for step in (1, 2, 3):
        scan_z(step).wait_recv()
    for h in range(NH):
        half = join(prefix(z, 2, h), prefix(y, -1, h))[1]
        entry[h, half_rows, :] = half
        end_out[h] = half.astype(BF)
    scan_end().start()

    for second in (0, 1):
        x_forward(second).wait_recv()
        side_pass(1, second).start()
    for p in (2, 3):
        side_pass(p, 0).wait_recv()
        side_pass(p, 1).wait_recv()
        to_twin(p).start()

    window(0)

    scan_end().wait_recv()
    for h in range(NH):
        entry[h, other_rows, :] = end_in[h].astype(F32)
        before = get_log(full_in.at[h, 128:144]), full_in[h, 0:HD, :].astype(F32)
        before = masked(1.0 - first_core, before)
        entering = jnp.exp(before[0]) * entry[h, 0:HD, :] + before[1]
        for f in range(FR):
            entering = decay(f, h) * entering
            sloc[f, h] = sloc[f, h] + entering

    def swap(p):
        mixed = qbuf.at[frame_of(p)]
        if p == 1:
            return remote(SWAP + 2, mixed, relay, onward)
        return remote(SWAP + p - 2, mixed, mixb.at[pl.ds(p * GP, GW)], x_peer(4 - RELS[p]))

    def swap_onward():
        return remote(SWAP + 3, relay, mixb.at[pl.ds(GP, GW)], onward)

    def attend(p):
        f = frame_of(p)
        for h in range(NH):
            rows = slice(h * HD, (h + 1) * HD)
            state = jnp.zeros((HD, HD), F32)
            for g in range(FR):
                state = state + flag(last_ref[f] == FR * tm + g) * sloc[g, h]
            linear = exact(state.astype(BF), qbuf[f, rows, :])
            inverse = lax.rsqrt(
                jnp.sum(linear * linear, axis=0, keepdims=True) * (1.0 / HD) + EPS
            )
            both = (linear * inverse + win[f, rows, :].astype(F32)).astype(BF)
            if p == 0:
                mixb[rows, :] = both
            else:
                qbuf[f, rows, :] = both

    for p in (1, 2, 3):
        attend(p)
        swap(p).start()
    attend(0)
    swap(1).wait_recv()
    swap_onward().start()
    side_pass(1, 0).wait_recv()
    side_pass(1, 1).wait_recv()
    to_twin(1).start()

    load_resid.wait()

    def weights(i, p, count):
        return wo[i, :, :, p * GP : (p + count) * GP].reshape(2 * PART, count * GP)

    for i in range(4):
        low, high = i * 2 * PART, min((i + 1) * 2 * PART, D)
        acc[low:high, :] = exact(weights(i, 0, 1)[: high - low], mixb[0:GP, :])

    for p in (2, 3):
        to_twin(p).wait_recv()
        swap(p).wait_recv()
    for i in range(4):
        low, high = i * 2 * PART, min((i + 1) * 2 * PART, D)
        acc[low:high, :] += exact(weights(i, 2, 2)[: high - low], mixb[2 * GP : 4 * GP, :])

    def store(i):
        rows = pl.ds(i * 2 * PART, min(2 * PART, D - i * 2 * PART))
        return load(9 + i, resid.at[rows], out_hbm.at[rows])

    to_twin(1).wait_recv()
    swap_onward().wait_recv()
    for i in range(4):
        low, high = i * 2 * PART, min((i + 1) * 2 * PART, D)
        total = acc[low:high, :] + exact(weights(i, 1, 1)[: high - low], mixb[GP : 2 * GP, :])
        for c in range(ROWS // 128):
            cols = slice(c * 128, (c + 1) * 128)
            resid[low:high, cols] = (
                resid[low:high, cols].astype(F32) + gains[low:high, 256:384] * total[:, cols]
            ).astype(BF)
        store(i).start()

    for p in (1, 2, 3):
        to_twin(p).wait_send()
        swap(p).wait_send()
        scan_y(p).wait_send()
        scan_z(p).wait_send()
    for second in (0, 1):
        for p in (1, 2, 3):
            side_pass(p, second).wait_send()
            if p > 1:
                x_gather(p, second).wait_send()
        x_forward(second).wait_send()
    swap_onward().wait_send()
    scan_core().wait_send()
    scan_end().wait_send()

    @pl.when(tm > 0)
    def _():
        halo_left().wait_send()

    @pl.when(tm < 31)
    def _():
        halo_right().wait_send()

    for i in range(4):
        store(i).wait()


def body(
    tokens, mod_scale, mod_shift, out_gate, w_query, w_key, w_value, w_out,
    log_decay, mix_weight, block_last, win_list,
):
    anywhere = pl.BlockSpec(memory_space=pl.ANY)
    vmem = pl.BlockSpec(memory_space=pltpu.VMEM)
    smem = pl.BlockSpec(memory_space=pltpu.SMEM)
    out = pl.pallas_call(
        kernel,
        out_shape=jax.ShapeDtypeStruct((D, ROWS), BF),
        in_specs=[anywhere, vmem, vmem, vmem] + [anywhere] * 4 + [vmem, smem, smem, vmem],
        out_specs=anywhere,
        scratch_shapes=[
            pltpu.VMEM((FR, D, ROWS), BF),
            pltpu.VMEM((D, ROWS), BF),
            pltpu.VMEM((3, GW, D), BF),
            pltpu.VMEM((GP, D), BF),
            pltpu.VMEM((4, 2, PART, 4 * GP), BF),
            pltpu.VMEM((2 * FR, GW, ROWS), BF),
            pltpu.VMEM((GW, ROWS), BF),
            pltpu.VMEM((FR, GW, ROWS), BF),
            pltpu.VMEM((FR, GW, ROWS), BF),
            pltpu.VMEM((4 * GP, ROWS), BF),
            pltpu.VMEM((D, ROWS), F32),
            pltpu.VMEM((D, 384), F32),
            pltpu.VMEM((GW, ROWS), BF),
            pltpu.VMEM((FR, NH, HD, HD), F32),
            pltpu.VMEM((NH, 128, HD), F32),
            pltpu.VMEM((NH, 128, HD), F32),
            pltpu.VMEM((NH, 144, HD), BF),
            pltpu.VMEM((NH, 144, HD), BF),
            pltpu.VMEM((2, NH * HALF + TT, HD), BF),
            pltpu.VMEM((6, NH * HALF + TT, HD), BF),
            pltpu.VMEM((NH, HALF, HD), BF),
            pltpu.VMEM((NH, HALF, HD), BF),
            pltpu.VMEM((NBR, TT, 128), F32),
            pltpu.VMEM((FR, NBR, ROWS), F32),
            pltpu.VMEM(((2 * WIN + 1) * 128, 128), BF),
            pltpu.SemaphoreType.DMA((13,)),
            pltpu.SemaphoreType.DMA((MESSAGES,)),
            pltpu.SemaphoreType.DMA((MESSAGES,)),
        ],
        compiler_params=pltpu.CompilerParams(
            collective_id=0, has_side_effects=True, vmem_limit_bytes=66_000_000
        ),
    )(
        tokens.T,
        mod_scale,
        mod_shift,
        out_gate,
        w_query.T,
        w_key.T,
        w_value.T,
        w_out,
        mix_weight.reshape(NBR * TT, TT),
        log_decay,
        block_last,
        win_list.transpose(1, 2, 0).reshape(TILES * NBR, -1),
    )
    return out.T


def solution(mesh):
    placed = (
        P("tm", None),
        P(),
        P(),
        P(),
        P(None, "space"),
        P(None, "space"),
        P(None, "space"),
        P("space", None),
        P("tm", "space"),
        P(),
        P("tm"),
        P(),
    )
    return jax.shard_map(
        body, mesh=mesh, in_specs=placed, out_specs=P(("tm", "space"), None), check_vma=False
    )
```

```python
import jax
import jax.numpy as jnp
from jax import lax
from jax.experimental import pallas as pl
from jax.experimental.pallas import tpu as pltpu
from jax.sharding import PartitionSpec as P

HD = 112
NH = 5
GW = NH * HD
GP = 640
D = 2240
FR = 4
ROWS = 512
TILES = 32
TT = 16
NBR = 8
WIN = 2
PART = 288
EPS = 1e-06
RELS = (0, 2, 3, 1)
MESH = pl.DeviceIdType.MESH
BF = jnp.bfloat16
F32 = jnp.float32
NT = (((1,), (1,)), ((), ()))

X_GATHER = 0
FORWARD = 4
SIDE_PASS = 6
TWIN = 12
HALO = 15
SCAN = 17
SWAP = 25
FAR = 29
MESSAGES = 35
HALF = 64


def kernel(
    tok_hbm, scale_ref, shift_ref, gate_ref, wq_hbm, wk_hbm, wv_hbm, wo_hbm, mix_ref,
    decay_ref, last_ref, list_ref, out_hbm,
    tok, resid, wqkv, wo_raw, wo, vbuf, kbuf, qbuf, win, mixb, acc, gains,
    relay, distant, states_out, states_relay, states_in, sloc, scur, entry, full_out, full_in, half_out, half_in, end_out, end_in,
    mixrep, rel, band, local_sem, send_sem, recv_sem,
):
    tm = lax.axis_index("tm")
    sp = lax.axis_index("space")
    z, y, core = tm // 8, (tm // 2) % 4, tm % 2

    def at(zz, yy, cc):
        return (zz * 8 + yy * 2 + cc, sp)

    def x_peer(step):
        return (tm, (sp + step) % 4)

    def z_peer(step):
        return at((z + step) % 4, y, core)

    def y_peer(step):
        return at(z, (y + step) % 4, core)

    twin = at(z, y, 1 - core)
    right = ((tm + 1) % 32, sp)
    left = ((tm + 31) % 32, sp)
    outer = ((tm + 31 + 2 * core) % 32, sp)

    def remote(number, src, dst, device):
        return pltpu.make_async_remote_copy(
            src_ref=src,
            dst_ref=dst,
            send_sem=send_sem.at[number],
            recv_sem=recv_sem.at[number],
            device_id=device,
            device_id_type=MESH,
        )

    def load(number, src, dst):
        return pltpu.make_async_copy(src, dst, local_sem.at[number])

    load_wo = load(0, wo_hbm, wo_raw.at[pl.ds(0, GW)])
    load_wv = load(1, wv_hbm, wqkv.at[0])
    load_wk = load(2, wk_hbm, wqkv.at[1])
    load_wq = load(3, wq_hbm, wqkv.at[2])
    own_rows = pl.ds(pl.multiple_of(sp * ROWS, ROWS), ROWS)
    load_resid = load(4, tok_hbm.at[:, own_rows], resid)

    def load_tok(f):
        rows = pl.ds(pl.multiple_of(f * ROWS, ROWS), ROWS)
        return load(5 + f, tok_hbm.at[:, rows], tok.at[f])

    load_wo.start()
    load_tok(0).start()
    load_wv.start()
    for f in range(1, FR):
        load_tok(f).start()
    load_wk.start()
    load_wq.start()
    load_resid.start()

    barrier = pltpu.get_barrier_semaphore()
    partners = [x_peer(i) for i in (1, 3)] + [y_peer(i) for i in (1, 2, 3)]
    partners += [z_peer(i) for i in (1, 2, 3)] + [twin, outer]
    for device in partners:
        pl.semaphore_signal(barrier, inc=1, device_id=device, device_id_type=MESH)

    def spots(rows, lanes, of_row, of_lane):
        r = lax.broadcasted_iota(jnp.int32, (rows, lanes), 0)
        l = lax.broadcasted_iota(jnp.int32, (rows, lanes), 1)
        return jnp.where(of_row(r) == of_lane(l), 1.0, 0.0).astype(BF)

    def exact(a, b, dims=(((1,), (0,)), ((), ()))):
        return lax.dot_general(a, b, dims, preferred_element_type=F32)

    for p in range(4):
        mixb[p * GP + GW : (p + 1) * GP, :] = jnp.zeros((GP - GW, ROWS), BF)

    wo_raw[GW:GP, :] = jnp.zeros((GP - GW, D), BF)
    wo[3, 1, D - 7 * PART : PART, 0:GP] = jnp.zeros((8 * PART - D, GP), BF)
    load_wo.wait()
    for low in range(0, D, 256):
        high = min(low + 256, D)
        eye = spots(high - low, high - low, lambda r: r, lambda l: l)
        turned = exact(eye, wo_raw[:, low:high], NT).astype(BF)
        for part in range(8):
            first, last = max(low, part * PART), min(high, (part + 1) * PART)
            if first < last:
                wo[part // 2, part % 2, first - part * PART : last - part * PART, 0:GP] = turned[
                    first - low : last - low
                ]

    pl.semaphore_wait(barrier, len(partners))

    def chunk(p, i):
        return wo.at[i, core, :, pl.ds(p * GP, GP)]

    onward = x_peer(1 + 2 * core)

    def place(p):
        if p == 2:
            return z, z_peer
        if p == 3:
            return y, y_peer
        return z + core * (y - z), lambda step: at(
            (z + (1 - core) * step) % 4, (y + core * step) % 4, core
        )

    def x_gather(p, second):
        i = (place(p)[0] + second) % 4
        number = X_GATHER + (p - 2) * 2 + second
        return remote(number, chunk(0, i), chunk(p, i), x_peer(4 - RELS[p]))

    def x_forward(second):
        i = (place(1)[0] + second) % 4
        cols = pl.ds(pl.multiple_of((2 + core) * GP, 128), GP)
        return remote(FORWARD + second, wo.at[i, core, :, cols], chunk(1, i), onward)

    def side_pass(p, second):
        i, peer = place(p)
        ref = chunk(p, (i + second) % 4)
        return remote(SIDE_PASS + (p - 1) * 2 + second, ref, ref, peer(3 if second else 1))

    def x_arrived(second):
        for p in (2, 3):
            x_gather(p, second).wait_recv()
            side_pass(p, second).start()
        x_forward(second).start()

    def to_twin(p):
        ref = wo.at[:, core, :, pl.ds(p * GP, GP)]
        return remote(TWIN + p - 1, ref, ref, twin)

    for second in (0, 1):
        for p in (2, 3):
            x_gather(p, second).start()

    parts = []
    for vector in (1.0 + scale_ref[...], shift_ref[...], gate_ref[...]):
        rest = vector.reshape(1, D)
        for _ in range(3):
            part = rest.astype(BF)
            parts.append(part)
            rest = rest - part.astype(F32)
    parts = jnp.concatenate(parts + [jnp.zeros((7, D), BF)], axis=0)
    gains[...] = exact(
        parts, spots(16, 384, lambda r: r // 3, lambda l: l // 128), (((0,), (0,)), ((), ()))
    )

    def norm(f):
        rows = 32

        def squares(i, total):
            x = tok[f, pl.ds(pl.multiple_of(i * rows, rows), rows), :].astype(F32)
            return total + jnp.sum((x * x).reshape(rows // 8, 8, ROWS), axis=0)

        total = lax.fori_loop(0, D // rows, squares, jnp.zeros((8, ROWS), F32), unroll=2)
        inverse = lax.rsqrt(jnp.sum(total, axis=0, keepdims=True) * (1.0 / D) + EPS)

        def scale(i, _):
            r = pl.ds(pl.multiple_of(i * rows, rows), rows)
            gain, shift = gains[r, 0:128], gains[r, 128:256]
            for c in range(ROWS // 128):
                cols = slice(c * 128, (c + 1) * 128)
                x = tok[f, r, cols].astype(F32)
                tok[f, r, cols] = (x * inverse[:, cols] * gain + shift).astype(BF)
            return 0

        lax.fori_loop(0, D // rows, scale, 0, unroll=2)

    def halo_left():
        return remote(HALO, vbuf.at[pl.ds(2, 2)], vbuf.at[pl.ds(6, 2)], left)

    def halo_right():
        return remote(HALO + 1, vbuf.at[pl.ds(4, 2)], vbuf.at[pl.ds(0, 2)], right)

    def decay(f, h):
        return jnp.exp(jnp.full((1, HD), decay_ref[f, h], F32))

    def project(weight, f, dst):
        for half in range(2):
            cols = slice(half * 256, (half + 1) * 256)
            dst[:, cols] = jnp.dot(
                wqkv[weight], tok[f, :, cols], preferred_element_type=F32
            ).astype(BF)

    @pl.when(tm == 0)
    def _():
        vbuf[0:2] = jnp.zeros((2, GW, ROWS), BF)

    @pl.when(tm == 31)
    def _():
        vbuf[6:8] = jnp.zeros((2, GW, ROWS), BF)

    load_wv.wait()

    def value(f, _):
        load_tok(f).wait()
        norm(f)
        project(0, f, vbuf.at[2 + f])

        @pl.when(f == 1)
        def _():
            @pl.when(tm > 0)
            def _():
                halo_left().start()

        @pl.when(f == 2)
        def _():
            x_arrived(0)

        @pl.when(f == 3)
        def _():
            @pl.when(tm < 31)
            def _():
                halo_right().start()

        return 0

    lax.fori_loop(0, FR, value, 0)

    load_wk.wait()
    scur[...] = jnp.zeros_like(scur)

    def key(f, _):
        project(1, f, kbuf)
        for h in range(NH):
            rows = slice(h * HD, (h + 1) * HD)
            fresh = exact(vbuf[2 + f, rows, :], kbuf[rows, :], NT)
            state = decay(f, h) * scur[h, 0:HD, :] + fresh
            scur[h, 0:HD, :] = state
            sloc[f, h] = state

        @pl.when(f == 1)
        def _():
            x_arrived(1)

        return 0

    lax.fori_loop(0, FR, key, 0)

    row_id = lax.broadcasted_iota(jnp.int32, (TT, HD), 0)
    half_rows = pl.ds(pl.multiple_of(core * HALF, HALF), HALF)
    other_rows = pl.ds(pl.multiple_of((1 - core) * HALF, HALF), HALF)

    def put_log(ref, log):
        high = log.astype(BF).astype(F32)
        low = log - high
        ref[...] = jnp.where(row_id == 0, high, jnp.where(row_id == 1, low, 0.0)).astype(BF)

    def get_log(ref):
        return jnp.sum(ref[...].astype(F32), axis=0, keepdims=True)

    def flag(condition):
        return jnp.where(condition, 1.0, 0.0).astype(F32)

    def join(early, late):
        return early[0] + late[0], jnp.exp(late[0]) * early[1] + late[1]

    def choose(on, pair, other):
        return tuple(on * a + (1.0 - on) * b for a, b in zip(pair, other))

    def masked(on, pair):
        return tuple(on * a for a in pair)

    def own_log(h):
        log = jnp.full((1, HD), decay_ref[0, h], F32)
        for f in range(1, FR):
            log = log + jnp.full((1, HD), decay_ref[f, h], F32)
        return log

    first_core = flag(core == 0)

    def chip_pair(h):
        own = own_log(h), scur[h, half_rows, :]
        other = get_log(full_in.at[h, 128:144]), full_in[h, half_rows, :].astype(F32)
        return join(choose(first_core, own, other), choose(first_core, other, own))

    def put(slot, pairs):
        logs = jnp.zeros((TT, HD), F32)
        for h, (log, state) in enumerate(pairs):
            half_out[slot, h * HALF : (h + 1) * HALF, :] = state.astype(BF)
            high = log.astype(BF).astype(F32)
            logs = jnp.where(row_id == 2 * h, high, logs)
            logs = jnp.where(row_id == 2 * h + 1, log - high, logs)
        half_out[slot, NH * HALF :, :] = logs.astype(BF)

    def get(slot, h):
        logs = half_in[slot, NH * HALF :, :].astype(F32)
        log = jnp.sum(jnp.where(row_id // 2 == h, logs, 0.0), axis=0, keepdims=True)
        return log, half_in[slot, h * HALF : (h + 1) * HALF, :].astype(F32)

    def scan_core():
        return remote(SCAN, full_out, full_in, twin)

    def scan_y(step):
        return remote(SCAN + step, half_out.at[0], half_in.at[step - 1], y_peer(step))

    def scan_z(step):
        return remote(SCAN + 3 + step, half_out.at[1], half_in.at[2 + step], z_peer(step))

    def scan_end():
        return remote(SCAN + 7, end_out, end_in, twin)

    def prefix(place, slot, h):
        total = None
        for step in (3, 2, 1):
            pair = masked(flag(place >= step), get(slot + step, h))
            total = pair if total is None else join(total, pair)
        return total

    for h in range(NH):
        full_out[h, 0:128, :] = scur[h].astype(BF)
        put_log(full_out.at[h, 128:144], own_log(h))
    scan_core().start()

    def frame_of(p):
        return (sp + 4 - RELS[p]) % 4

    load_wq.wait()

    def query(p):
        project(2, frame_of(p), qbuf.at[frame_of(p)])

    def far(kind, leg):
        if kind == 0:
            refs = qbuf.at[frame_of(1)], relay.at[0], distant.at[0]
        elif kind == 1:
            refs = win.at[frame_of(1)], relay.at[1], distant.at[1]
        else:
            refs = states_out, states_relay, states_in
        return remote(FAR + kind * 2 + leg, refs[leg], refs[leg + 1], onward)

    query(1)
    far(0, 0).start()

    scan_core().wait_recv()
    put(0, [chip_pair(h) for h in range(NH)])
    for step in (1, 2, 3):
        scan_y(step).start()

    query(2)
    mixed_t = exact(spots(TT, TT, lambda r: r, lambda l: l), mix_ref[...], NT).astype(BF)
    mine = exact(
        spots(8, 128, lambda r: r + FR * tm, lambda l: l), list_ref[...].astype(BF), NT
    )
    mine = (mine - (FR * tm - WIN).astype(F32)).astype(BF)
    for n in range(NBR):
        mixrep[n] = exact(
            mixed_t, spots(128, 128, lambda r: r, lambda l: l % TT + n * TT)
        )
        listed = exact(
            mine, spots(TILES * NBR, ROWS, lambda r: r, lambda l: l // TT * NBR + n)
        )
        for f in range(FR):
            rel[f, n : n + 1, :] = listed[f : f + 1]

    query(3)
    far(0, 0).wait_recv()
    far(0, 1).start()

    @pl.when(tm < 31)
    def _():
        halo_left().wait_recv()

    @pl.when(tm > 0)
    def _():
        halo_right().wait_recv()

    tile_of_lane = lax.broadcasted_iota(jnp.int32, (TT, 128), 1) // TT

    def window(p):
        f = frame_of(p)

        def tiles(j, _):
            cols = pl.ds(pl.multiple_of(j * 128, 128), 128)
            for g in range(2 * WIN + 1):
                block = jnp.zeros((TT, 128), F32)
                for n in range(NBR):
                    listed = rel[f, n : n + 1, cols]
                    block = block + jnp.where(listed == (f + g).astype(F32), mixrep[n], 0.0)
                for t in range(8):
                    low = g * 128 + t * TT
                    band[low : low + TT, :] = jnp.where(tile_of_lane == t, block, 0.0).astype(BF)
            source = jnp.concatenate([vbuf[f + g, :, cols] for g in range(2 * WIN + 1)], axis=1)
            win[f, :, cols] = exact(source, band[...]).astype(BF)
            return 0

        lax.fori_loop(0, ROWS // 128, tiles, 0)

    window(1)
    far(1, 0).start()

    for step in (1, 2, 3):
        scan_y(step).wait_recv()
    totals = []
    for h in range(NH):
        total = join(prefix(y, -1, h), chip_pair(h))
        for step in (3, 2, 1):
            total = join(total, masked(flag(y < step), get(step - 1, h)))
        totals.append(total)
    put(1, totals)
    for step in (1, 2, 3):
        scan_z(step).start()

    window(2)
    query(0)
    window(3)
    far(1, 0).wait_recv()
    far(1, 1).start()

    for step in (1, 2, 3):
        scan_z(step).wait_recv()
    for h in range(NH):
        half = join(prefix(z, 2, h), prefix(y, -1, h))[1]
        entry[h, half_rows, :] = half
        end_out[h] = half.astype(BF)
    scan_end().start()

    for second in (0, 1):
        x_forward(second).wait_recv()
        side_pass(1, second).start()
    for p in (2, 3):
        side_pass(p, 0).wait_recv()
        side_pass(p, 1).wait_recv()
        to_twin(p).start()

    window(0)

    scan_end().wait_recv()
    for h in range(NH):
        entry[h, other_rows, :] = end_in[h].astype(F32)
        before = get_log(full_in.at[h, 128:144]), full_in[h, 0:HD, :].astype(F32)
        before = masked(1.0 - first_core, before)
        entering = jnp.exp(before[0]) * entry[h, 0:HD, :] + before[1]
        for f in range(FR):
            entering = decay(f, h) * entering
            sloc[f, h] = sloc[f, h] + entering

    def state_of(p, h):
        state = jnp.zeros((HD, HD), F32)
        for g in range(FR):
            state = state + flag(last_ref[frame_of(p)] == FR * tm + g) * sloc[g, h]
        return state.astype(BF)

    def attend(state, query_ref, window_ref, out_ref, h, cols):
        rows = slice(h * HD, (h + 1) * HD)
        linear = exact(state, query_ref[rows, cols])
        inverse = lax.rsqrt(jnp.sum(linear * linear, axis=0, keepdims=True) * (1.0 / HD) + EPS)
        out_ref[rows, cols] = (linear * inverse + window_ref[rows, cols].astype(F32)).astype(BF)

    def half_cols(half):
        return pl.ds(half * 256, 256)

    def swap(p, half):
        return remote(
            SWAP + (p - 2) * 2 + half,
            qbuf.at[frame_of(p), :, half_cols(half)],
            mixb.at[pl.ds(p * GP, GW), half_cols(half)],
            x_peer(4 - RELS[p]),
        )

    for h in range(NH):
        states_out[h] = state_of(1, h)
    far(2, 0).start()
    for half in range(2):
        for p in (2, 3):
            f = frame_of(p)
            for h in range(NH):
                attend(state_of(p, h), qbuf.at[f], win.at[f], qbuf.at[f], h, half_cols(half))
            swap(p, half).start()
    far(2, 0).wait_recv()
    far(2, 1).start()
    for h in range(NH):
        f = frame_of(0)
        attend(state_of(0, h), qbuf.at[f], win.at[f], mixb.at[pl.ds(0, GW)], h, slice(0, ROWS))
    side_pass(1, 0).wait_recv()
    side_pass(1, 1).wait_recv()
    to_twin(1).start()

    load_resid.wait()

    def weights(i, p, count):
        return wo[i, :, :, p * GP : (p + count) * GP].reshape(2 * PART, count * GP)

    for i in range(4):
        low, high = i * 2 * PART, min((i + 1) * 2 * PART, D)
        acc[low:high, :] = exact(weights(i, 0, 1)[: high - low], mixb[0:GP, :])

    for kind in range(3):
        far(kind, 1).wait_recv()
    for h in range(NH):
        attend(
            states_in[h], distant.at[0], distant.at[1], mixb.at[pl.ds(GP, GW)], h, slice(0, ROWS)
        )
    to_twin(1).wait_recv()
    for i in range(4):
        low, high = i * 2 * PART, min((i + 1) * 2 * PART, D)
        acc[low:high, :] += exact(weights(i, 1, 1)[: high - low], mixb[GP : 2 * GP, :])

    def store(i, half):
        rows = pl.ds(i * 2 * PART, min(2 * PART, D - i * 2 * PART))
        cols = half_cols(half)
        return load(9 + i + 4 * half, resid.at[rows, cols], out_hbm.at[rows, cols])

    for p in (2, 3):
        to_twin(p).wait_recv()
    for half in range(2):
        for p in (2, 3):
            swap(p, half).wait_recv()
        near = slice(half * 256, (half + 1) * 256)
        for i in range(4):
            low, high = i * 2 * PART, min((i + 1) * 2 * PART, D)
            total = acc[low:high, near] + exact(
                weights(i, 2, 2)[: high - low], mixb[2 * GP : 4 * GP, near]
            )
            for c in range(2):
                cols = slice(half * 256 + c * 128, half * 256 + (c + 1) * 128)
                resid[low:high, cols] = (
                    resid[low:high, cols].astype(F32)
                    + gains[low:high, 256:384] * total[:, c * 128 : (c + 1) * 128]
                ).astype(BF)
            store(i, half).start()

    for p in (1, 2, 3):
        to_twin(p).wait_send()
        scan_y(p).wait_send()
        scan_z(p).wait_send()
    for second in (0, 1):
        for p in (1, 2, 3):
            side_pass(p, second).wait_send()
            if p > 1:
                x_gather(p, second).wait_send()
        x_forward(second).wait_send()
    for half in range(2):
        for p in (2, 3):
            swap(p, half).wait_send()
    for kind in range(3):
        for leg in range(2):
            far(kind, leg).wait_send()
    scan_core().wait_send()
    scan_end().wait_send()

    @pl.when(tm > 0)
    def _():
        halo_left().wait_send()

    @pl.when(tm < 31)
    def _():
        halo_right().wait_send()

    for half in range(2):
        for i in range(4):
            store(i, half).wait()


def body(
    tokens, mod_scale, mod_shift, out_gate, w_query, w_key, w_value, w_out,
    log_decay, mix_weight, block_last, win_list,
):
    anywhere = pl.BlockSpec(memory_space=pl.ANY)
    vmem = pl.BlockSpec(memory_space=pltpu.VMEM)
    smem = pl.BlockSpec(memory_space=pltpu.SMEM)
    out = pl.pallas_call(
        kernel,
        out_shape=jax.ShapeDtypeStruct((D, ROWS), BF),
        in_specs=[anywhere, vmem, vmem, vmem] + [anywhere] * 4 + [vmem, smem, smem, vmem],
        out_specs=anywhere,
        scratch_shapes=[
            pltpu.VMEM((FR, D, ROWS), BF),
            pltpu.VMEM((D, ROWS), BF),
            pltpu.VMEM((3, GW, D), BF),
            pltpu.VMEM((GP, D), BF),
            pltpu.VMEM((4, 2, PART, 4 * GP), BF),
            pltpu.VMEM((2 * FR, GW, ROWS), BF),
            pltpu.VMEM((GW, ROWS), BF),
            pltpu.VMEM((FR, GW, ROWS), BF),
            pltpu.VMEM((FR, GW, ROWS), BF),
            pltpu.VMEM((4 * GP, ROWS), BF),
            pltpu.VMEM((D, ROWS), F32),
            pltpu.VMEM((D, 384), F32),
            pltpu.VMEM((2, GW, ROWS), BF),
            pltpu.VMEM((2, GW, ROWS), BF),
            pltpu.VMEM((NH, HD, HD), BF),
            pltpu.VMEM((NH, HD, HD), BF),
            pltpu.VMEM((NH, HD, HD), BF),
            pltpu.VMEM((FR, NH, HD, HD), F32),
            pltpu.VMEM((NH, 128, HD), F32),
            pltpu.VMEM((NH, 128, HD), F32),
            pltpu.VMEM((NH, 144, HD), BF),
            pltpu.VMEM((NH, 144, HD), BF),
            pltpu.VMEM((2, NH * HALF + TT, HD), BF),
            pltpu.VMEM((6, NH * HALF + TT, HD), BF),
            pltpu.VMEM((NH, HALF, HD), BF),
            pltpu.VMEM((NH, HALF, HD), BF),
            pltpu.VMEM((NBR, TT, 128), F32),
            pltpu.VMEM((FR, NBR, ROWS), F32),
            pltpu.VMEM(((2 * WIN + 1) * 128, 128), BF),
            pltpu.SemaphoreType.DMA((17,)),
            pltpu.SemaphoreType.DMA((MESSAGES,)),
            pltpu.SemaphoreType.DMA((MESSAGES,)),
        ],
        compiler_params=pltpu.CompilerParams(
            collective_id=0, has_side_effects=True, vmem_limit_bytes=66_000_000
        ),
    )(
        tokens.T,
        mod_scale,
        mod_shift,
        out_gate,
        w_query.T,
        w_key.T,
        w_value.T,
        w_out,
        mix_weight.reshape(NBR * TT, TT),
        log_decay,
        block_last,
        win_list.transpose(1, 2, 0).reshape(TILES * NBR, -1),
    )
    return out.T


def solution(mesh):
    placed = (
        P("tm", None),
        P(),
        P(),
        P(),
        P(None, "space"),
        P(None, "space"),
        P(None, "space"),
        P("space", None),
        P("tm", "space"),
        P(),
        P("tm"),
        P(),
    )
    return jax.shard_map(
        body, mesh=mesh, in_specs=placed, out_specs=P(("tm", "space"), None), check_vma=False
    )
```

```python
import jax
import jax.numpy as jnp
from jax import lax
from jax.experimental import pallas as pl
from jax.experimental.pallas import tpu as pltpu
from jax.sharding import PartitionSpec as P

HD = 112
NH = 5
GW = NH * HD
GP = 640
D = 2240
FR = 4
ROWS = 512
TILES = 32
TT = 16
NBR = 8
WIN = 2
PART = 288
EPS = 1e-06
RELS = (0, 2, 3, 1)
MESH = pl.DeviceIdType.MESH
BF = jnp.bfloat16
F32 = jnp.float32
NT = (((1,), (1,)), ((), ()))

X_GATHER = 0
FORWARD = 4
SIDE_PASS = 6
TWIN = 12
HALO = 15
SCAN = 17
SWAP = 25
MESSAGES = 31
HALF = 64


def kernel(
    tok_hbm, scale_ref, shift_ref, gate_ref, wq_hbm, wk_hbm, wv_hbm, wo_hbm, mix_ref,
    decay_ref, last_ref, list_ref, out_hbm,
    tok, resid, wqkv, wo_raw, wo, vbuf, kbuf, qbuf, win, mixb, acc, gains,
    relay, sloc, scur, entry, full_out, full_in, half_out, half_in, end_out, end_in,
    mixrep, rel, band, local_sem, send_sem, recv_sem,
):
    tm = lax.axis_index("tm")
    sp = lax.axis_index("space")
    z, y, core = tm // 8, (tm // 2) % 4, tm % 2

    def at(zz, yy, cc):
        return (zz * 8 + yy * 2 + cc, sp)

    def x_peer(step):
        return (tm, (sp + step) % 4)

    def z_peer(step):
        return at((z + step) % 4, y, core)

    def y_peer(step):
        return at(z, (y + step) % 4, core)

    twin = at(z, y, 1 - core)
    right = ((tm + 1) % 32, sp)
    left = ((tm + 31) % 32, sp)
    outer = ((tm + 31 + 2 * core) % 32, sp)

    def remote(number, src, dst, device):
        return pltpu.make_async_remote_copy(
            src_ref=src,
            dst_ref=dst,
            send_sem=send_sem.at[number],
            recv_sem=recv_sem.at[number],
            device_id=device,
            device_id_type=MESH,
        )

    def load(number, src, dst):
        return pltpu.make_async_copy(src, dst, local_sem.at[number])

    load_wo = load(0, wo_hbm, wo_raw.at[pl.ds(0, GW)])
    load_wv = load(1, wv_hbm, wqkv.at[0])
    load_wk = load(2, wk_hbm, wqkv.at[1])
    load_wq = load(3, wq_hbm, wqkv.at[2])
    own_rows = pl.ds(pl.multiple_of(sp * ROWS, ROWS), ROWS)
    load_resid = load(4, tok_hbm.at[:, own_rows], resid)

    def load_tok(f):
        rows = pl.ds(pl.multiple_of(f * ROWS, ROWS), ROWS)
        return load(5 + f, tok_hbm.at[:, rows], tok.at[f])

    load_wo.start()
    load_tok(0).start()
    load_wv.start()
    for f in range(1, FR):
        load_tok(f).start()
    load_wk.start()
    load_wq.start()
    load_resid.start()

    barrier = pltpu.get_barrier_semaphore()
    partners = [x_peer(i) for i in (1, 3)] + [y_peer(i) for i in (1, 2, 3)]
    partners += [z_peer(i) for i in (1, 2, 3)] + [twin, outer]
    for device in partners:
        pl.semaphore_signal(barrier, inc=1, device_id=device, device_id_type=MESH)

    def spots(rows, lanes, of_row, of_lane):
        r = lax.broadcasted_iota(jnp.int32, (rows, lanes), 0)
        l = lax.broadcasted_iota(jnp.int32, (rows, lanes), 1)
        return jnp.where(of_row(r) == of_lane(l), 1.0, 0.0).astype(BF)

    def exact(a, b, dims=(((1,), (0,)), ((), ()))):
        return lax.dot_general(a, b, dims, preferred_element_type=F32)

    for p in range(4):
        mixb[p * GP + GW : (p + 1) * GP, :] = jnp.zeros((GP - GW, ROWS), BF)

    wo_raw[GW:GP, :] = jnp.zeros((GP - GW, D), BF)
    wo[3, 1, D - 7 * PART : PART, 0:GP] = jnp.zeros((8 * PART - D, GP), BF)
    load_wo.wait()
    for low in range(0, D, 256):
        high = min(low + 256, D)
        eye = spots(high - low, high - low, lambda r: r, lambda l: l)
        turned = exact(eye, wo_raw[:, low:high], NT).astype(BF)
        for part in range(8):
            first, last = max(low, part * PART), min(high, (part + 1) * PART)
            if first < last:
                wo[part // 2, part % 2, first - part * PART : last - part * PART, 0:GP] = turned[
                    first - low : last - low
                ]

    pl.semaphore_wait(barrier, len(partners))

    def chunk(p, i):
        return wo.at[i, core, :, pl.ds(p * GP, GP)]

    onward = x_peer(1 + 2 * core)

    def place(p):
        if p == 2:
            return z, z_peer
        if p == 3:
            return y, y_peer
        return z + core * (y - z), lambda step: at(
            (z + (1 - core) * step) % 4, (y + core * step) % 4, core
        )

    def x_gather(p, second):
        i = (place(p)[0] + second) % 4
        number = X_GATHER + (p - 2) * 2 + second
        return remote(number, chunk(0, i), chunk(p, i), x_peer(4 - RELS[p]))

    def x_forward(second):
        i = (place(1)[0] + second) % 4
        cols = pl.ds(pl.multiple_of((2 + core) * GP, 128), GP)
        return remote(FORWARD + second, wo.at[i, core, :, cols], chunk(1, i), onward)

    def side_pass(p, second):
        i, peer = place(p)
        ref = chunk(p, (i + second) % 4)
        return remote(SIDE_PASS + (p - 1) * 2 + second, ref, ref, peer(3 if second else 1))

    def x_arrived(second):
        for p in (2, 3):
            x_gather(p, second).wait_recv()
            side_pass(p, second).start()
        x_forward(second).start()

    def to_twin(p):
        ref = wo.at[:, core, :, pl.ds(p * GP, GP)]
        return remote(TWIN + p - 1, ref, ref, twin)

    for second in (0, 1):
        for p in (2, 3):
            x_gather(p, second).start()

    parts = []
    for vector in (1.0 + scale_ref[...], shift_ref[...], gate_ref[...]):
        rest = vector.reshape(1, D)
        for _ in range(3):
            part = rest.astype(BF)
            parts.append(part)
            rest = rest - part.astype(F32)
    parts = jnp.concatenate(parts + [jnp.zeros((7, D), BF)], axis=0)
    gains[...] = exact(
        parts, spots(16, 384, lambda r: r // 3, lambda l: l // 128), (((0,), (0,)), ((), ()))
    )

    def norm(f):
        rows = 32

        def squares(i, total):
            x = tok[f, pl.ds(pl.multiple_of(i * rows, rows), rows), :].astype(F32)
            return total + jnp.sum((x * x).reshape(rows // 8, 8, ROWS), axis=0)

        total = lax.fori_loop(0, D // rows, squares, jnp.zeros((8, ROWS), F32), unroll=2)
        inverse = lax.rsqrt(jnp.sum(total, axis=0, keepdims=True) * (1.0 / D) + EPS)

        def scale(i, _):
            r = pl.ds(pl.multiple_of(i * rows, rows), rows)
            gain, shift = gains[r, 0:128], gains[r, 128:256]
            for c in range(ROWS // 128):
                cols = slice(c * 128, (c + 1) * 128)
                x = tok[f, r, cols].astype(F32)
                tok[f, r, cols] = (x * inverse[:, cols] * gain + shift).astype(BF)
            return 0

        lax.fori_loop(0, D // rows, scale, 0, unroll=2)

    def halo_left():
        return remote(HALO, vbuf.at[pl.ds(2, 2)], vbuf.at[pl.ds(6, 2)], left)

    def halo_right():
        return remote(HALO + 1, vbuf.at[pl.ds(4, 2)], vbuf.at[pl.ds(0, 2)], right)

    def decay(f, h):
        return jnp.exp(jnp.full((1, HD), decay_ref[f, h], F32))

    def project(weight, f, dst):
        dst[...] = exact(wqkv[weight], tok[f]).astype(BF)

    @pl.when(tm == 0)
    def _():
        vbuf[0:2] = jnp.zeros((2, GW, ROWS), BF)

    @pl.when(tm == 31)
    def _():
        vbuf[6:8] = jnp.zeros((2, GW, ROWS), BF)

    load_wv.wait()

    def value(f, _):
        load_tok(f).wait()
        norm(f)
        project(0, f, vbuf.at[2 + f])

        @pl.when(f == 1)
        def _():
            @pl.when(tm > 0)
            def _():
                halo_left().start()

        @pl.when(f == 2)
        def _():
            x_arrived(0)

        @pl.when(f == 3)
        def _():
            @pl.when(tm < 31)
            def _():
                halo_right().start()

        return 0

    lax.fori_loop(0, FR, value, 0)

    load_wk.wait()
    scur[...] = jnp.zeros_like(scur)

    def key(f, _):
        project(1, f, kbuf)
        for h in range(NH):
            rows = slice(h * HD, (h + 1) * HD)
            fresh = exact(vbuf[2 + f, rows, :], kbuf[rows, :], NT)
            state = decay(f, h) * scur[h, 0:HD, :] + fresh
            scur[h, 0:HD, :] = state
            sloc[f, h] = state

        @pl.when(f == 3)
        def _():
            x_arrived(1)

        return 0

    lax.fori_loop(0, FR, key, 0)

    row_id = lax.broadcasted_iota(jnp.int32, (TT, HD), 0)
    half_rows = pl.ds(pl.multiple_of(core * HALF, HALF), HALF)
    other_rows = pl.ds(pl.multiple_of((1 - core) * HALF, HALF), HALF)

    def put_log(ref, log):
        high = log.astype(BF).astype(F32)
        low = log - high
        ref[...] = jnp.where(row_id == 0, high, jnp.where(row_id == 1, low, 0.0)).astype(BF)

    def get_log(ref):
        return jnp.sum(ref[...].astype(F32), axis=0, keepdims=True)

    def flag(condition):
        return jnp.where(condition, 1.0, 0.0).astype(F32)

    def join(early, late):
        return early[0] + late[0], jnp.exp(late[0]) * early[1] + late[1]

    def choose(on, pair, other):
        return tuple(on * a + (1.0 - on) * b for a, b in zip(pair, other))

    def masked(on, pair):
        return tuple(on * a for a in pair)

    def own_log(h):
        log = jnp.full((1, HD), decay_ref[0, h], F32)
        for f in range(1, FR):
            log = log + jnp.full((1, HD), decay_ref[f, h], F32)
        return log

    first_core = flag(core == 0)

    def chip_pair(h):
        own = own_log(h), scur[h, half_rows, :]
        other = get_log(full_in.at[h, 128:144]), full_in[h, half_rows, :].astype(F32)
        return join(choose(first_core, own, other), choose(first_core, other, own))

    def put(slot, pairs):
        logs = jnp.zeros((TT, HD), F32)
        for h, (log, state) in enumerate(pairs):
            half_out[slot, h * HALF : (h + 1) * HALF, :] = state.astype(BF)
            high = log.astype(BF).astype(F32)
            logs = jnp.where(row_id == 2 * h, high, logs)
            logs = jnp.where(row_id == 2 * h + 1, log - high, logs)
        half_out[slot, NH * HALF :, :] = logs.astype(BF)

    def get(slot, h):
        logs = half_in[slot, NH * HALF :, :].astype(F32)
        log = jnp.sum(jnp.where(row_id // 2 == h, logs, 0.0), axis=0, keepdims=True)
        return log, half_in[slot, h * HALF : (h + 1) * HALF, :].astype(F32)

    def scan_core():
        return remote(SCAN, full_out, full_in, twin)

    def scan_y(step):
        return remote(SCAN + step, half_out.at[0], half_in.at[step - 1], y_peer(step))

    def scan_z(step):
        return remote(SCAN + 3 + step, half_out.at[1], half_in.at[2 + step], z_peer(step))

    def scan_end():
        return remote(SCAN + 7, end_out, end_in, twin)

    def prefix(place, slot, h):
        total = None
        for step in (3, 2, 1):
            pair = masked(flag(place >= step), get(slot + step, h))
            total = pair if total is None else join(total, pair)
        return total

    for h in range(NH):
        full_out[h, 0:128, :] = scur[h].astype(BF)
        put_log(full_out.at[h, 128:144], own_log(h))
    scan_core().start()

    def frame_of(p):
        return (sp + 4 - RELS[p]) % 4

    load_wq.wait()

    def query(p):
        project(2, frame_of(p), qbuf.at[frame_of(p)])

    query(1)

    scan_core().wait_recv()
    put(0, [chip_pair(h) for h in range(NH)])
    for step in (1, 2, 3):
        scan_y(step).start()

    query(2)
    mixed_t = exact(spots(TT, TT, lambda r: r, lambda l: l), mix_ref[...], NT).astype(BF)
    mine = exact(
        spots(8, 128, lambda r: r + FR * tm, lambda l: l), list_ref[...].astype(BF), NT
    )
    mine = (mine - (FR * tm - WIN).astype(F32)).astype(BF)
    for n in range(NBR):
        mixrep[n] = exact(
            mixed_t, spots(128, 128, lambda r: r, lambda l: l % TT + n * TT)
        )
        listed = exact(
            mine, spots(TILES * NBR, ROWS, lambda r: r, lambda l: l // TT * NBR + n)
        )
        for f in range(FR):
            rel[f, n : n + 1, :] = listed[f : f + 1]

    query(3)
    query(0)

    for step in (1, 2, 3):
        scan_y(step).wait_recv()
    totals = []
    for h in range(NH):
        total = join(prefix(y, -1, h), chip_pair(h))
        for step in (3, 2, 1):
            total = join(total, masked(flag(y < step), get(step - 1, h)))
        totals.append(total)
    put(1, totals)
    for step in (1, 2, 3):
        scan_z(step).start()

    @pl.when(tm < 31)
    def _():
        halo_left().wait_recv()

    @pl.when(tm > 0)
    def _():
        halo_right().wait_recv()

    tile_of_lane = lax.broadcasted_iota(jnp.int32, (TT, 128), 1) // TT

    def window(p):
        f = frame_of(p)

        def tiles(j, _):
            cols = pl.ds(pl.multiple_of(j * 128, 128), 128)
            for g in range(2 * WIN + 1):
                block = jnp.zeros((TT, 128), F32)
                for n in range(NBR):
                    listed = rel[f, n : n + 1, cols]
                    block = block + jnp.where(listed == (f + g).astype(F32), mixrep[n], 0.0)
                for t in range(8):
                    low = g * 128 + t * TT
                    band[low : low + TT, :] = jnp.where(tile_of_lane == t, block, 0.0).astype(BF)
            source = jnp.concatenate([vbuf[f + g, :, cols] for g in range(2 * WIN + 1)], axis=1)
            win[f, :, cols] = exact(source, band[...]).astype(BF)
            return 0

        lax.fori_loop(0, ROWS // 128, tiles, 0)

    window(1)
    window(2)
    window(3)

    for step in (1, 2, 3):
        scan_z(step).wait_recv()
    for h in range(NH):
        half = join(prefix(z, 2, h), prefix(y, -1, h))[1]
        entry[h, half_rows, :] = half
        end_out[h] = half.astype(BF)
    scan_end().start()

    for second in (0, 1):
        x_forward(second).wait_recv()
        side_pass(1, second).start()
    for p in (2, 3):
        side_pass(p, 0).wait_recv()
        side_pass(p, 1).wait_recv()
        to_twin(p).start()

    window(0)

    scan_end().wait_recv()
    for h in range(NH):
        entry[h, other_rows, :] = end_in[h].astype(F32)
        before = get_log(full_in.at[h, 128:144]), full_in[h, 0:HD, :].astype(F32)
        before = masked(1.0 - first_core, before)
        entering = jnp.exp(before[0]) * entry[h, 0:HD, :] + before[1]
        for f in range(FR):
            entering = decay(f, h) * entering
            sloc[f, h] = sloc[f, h] + entering

    def swap(p):
        return remote(
            SWAP + p - 2,
            qbuf.at[frame_of(p)],
            mixb.at[pl.ds(p * GP, GW)],
            x_peer(4 - RELS[p]),
        )

    def far(leg, half):
        cols = pl.ds(half * 256, 256)
        refs = qbuf.at[frame_of(1), :, cols], relay.at[:, cols], mixb.at[pl.ds(GP, GW), cols]
        return remote(SWAP + 2 + leg * 2 + half, refs[leg], refs[leg + 1], onward)

    def attend(p, low=0, high=ROWS):
        f = frame_of(p)
        cols = slice(low, high)
        for h in range(NH):
            rows = slice(h * HD, (h + 1) * HD)
            state = jnp.zeros((HD, HD), F32)
            for g in range(FR):
                state = state + flag(last_ref[f] == FR * tm + g) * sloc[g, h]
            linear = exact(state.astype(BF), qbuf[f, rows, cols])
            inverse = lax.rsqrt(
                jnp.sum(linear * linear, axis=0, keepdims=True) * (1.0 / HD) + EPS
            )
            both = (linear * inverse + win[f, rows, cols].astype(F32)).astype(BF)
            if p == 0:
                mixb[rows, cols] = both
            else:
                qbuf[f, rows, cols] = both

    for half in range(2):
        attend(1, half * 256, (half + 1) * 256)
        far(0, half).start()
    for p in (2, 3):
        attend(p)
        swap(p).start()
    far(0, 0).wait_recv()
    far(1, 0).start()
    attend(0)
    far(0, 1).wait_recv()
    far(1, 1).start()
    side_pass(1, 0).wait_recv()
    side_pass(1, 1).wait_recv()
    to_twin(1).start()

    load_resid.wait()

    def weights(i, p, count):
        return wo[i, :, :, p * GP : (p + count) * GP].reshape(2 * PART, count * GP)

    for i in range(4):
        low, high = i * 2 * PART, min((i + 1) * 2 * PART, D)
        acc[low:high, :] = exact(weights(i, 0, 1)[: high - low], mixb[0:GP, :])

    for p in (2, 3):
        to_twin(p).wait_recv()
        swap(p).wait_recv()
    for i in range(4):
        low, high = i * 2 * PART, min((i + 1) * 2 * PART, D)
        acc[low:high, :] += exact(weights(i, 2, 2)[: high - low], mixb[2 * GP : 4 * GP, :])

    def store(i, half):
        rows = pl.ds(i * 2 * PART, min(2 * PART, D - i * 2 * PART))
        cols = pl.ds(half * 256, 256)
        return load(9 + i + 4 * half, resid.at[rows, cols], out_hbm.at[rows, cols])

    to_twin(1).wait_recv()
    for half in range(2):
        far(1, half).wait_recv()
        now = slice(half * 256, (half + 1) * 256)
        for i in range(4):
            low, high = i * 2 * PART, min((i + 1) * 2 * PART, D)
            total = acc[low:high, now] + exact(
                weights(i, 1, 1)[: high - low], mixb[GP : 2 * GP, now]
            )
            for c in range(2):
                cols = slice(half * 256 + c * 128, half * 256 + (c + 1) * 128)
                resid[low:high, cols] = (
                    resid[low:high, cols].astype(F32)
                    + gains[low:high, 256:384] * total[:, c * 128 : (c + 1) * 128]
                ).astype(BF)
            store(i, half).start()

    for p in (1, 2, 3):
        to_twin(p).wait_send()
        if p > 1:
            swap(p).wait_send()
        scan_y(p).wait_send()
        scan_z(p).wait_send()
    for second in (0, 1):
        for p in (1, 2, 3):
            side_pass(p, second).wait_send()
            if p > 1:
                x_gather(p, second).wait_send()
        x_forward(second).wait_send()
    for half in range(2):
        for leg in range(2):
            far(leg, half).wait_send()
    scan_core().wait_send()
    scan_end().wait_send()

    @pl.when(tm > 0)
    def _():
        halo_left().wait_send()

    @pl.when(tm < 31)
    def _():
        halo_right().wait_send()

    for half in range(2):
        for i in range(4):
            store(i, half).wait()


def body(
    tokens, mod_scale, mod_shift, out_gate, w_query, w_key, w_value, w_out,
    log_decay, mix_weight, block_last, win_list,
):
    anywhere = pl.BlockSpec(memory_space=pl.ANY)
    vmem = pl.BlockSpec(memory_space=pltpu.VMEM)
    smem = pl.BlockSpec(memory_space=pltpu.SMEM)
    out = pl.pallas_call(
        kernel,
        out_shape=jax.ShapeDtypeStruct((D, ROWS), BF),
        in_specs=[anywhere, vmem, vmem, vmem] + [anywhere] * 4 + [vmem, smem, smem, vmem],
        out_specs=anywhere,
        scratch_shapes=[
            pltpu.VMEM((FR, D, ROWS), BF),
            pltpu.VMEM((D, ROWS), BF),
            pltpu.VMEM((3, GW, D), BF),
            pltpu.VMEM((GP, D), BF),
            pltpu.VMEM((4, 2, PART, 4 * GP), BF),
            pltpu.VMEM((2 * FR, GW, ROWS), BF),
            pltpu.VMEM((GW, ROWS), BF),
            pltpu.VMEM((FR, GW, ROWS), BF),
            pltpu.VMEM((FR, GW, ROWS), BF),
            pltpu.VMEM((4 * GP, ROWS), BF),
            pltpu.VMEM((D, ROWS), F32),
            pltpu.VMEM((D, 384), F32),
            pltpu.VMEM((GW, ROWS), BF),
            pltpu.VMEM((FR, NH, HD, HD), F32),
            pltpu.VMEM((NH, 128, HD), F32),
            pltpu.VMEM((NH, 128, HD), F32),
            pltpu.VMEM((NH, 144, HD), BF),
            pltpu.VMEM((NH, 144, HD), BF),
            pltpu.VMEM((2, NH * HALF + TT, HD), BF),
            pltpu.VMEM((6, NH * HALF + TT, HD), BF),
            pltpu.VMEM((NH, HALF, HD), BF),
            pltpu.VMEM((NH, HALF, HD), BF),
            pltpu.VMEM((NBR, TT, 128), F32),
            pltpu.VMEM((FR, NBR, ROWS), F32),
            pltpu.VMEM(((2 * WIN + 1) * 128, 128), BF),
            pltpu.SemaphoreType.DMA((17,)),
            pltpu.SemaphoreType.DMA((MESSAGES,)),
            pltpu.SemaphoreType.DMA((MESSAGES,)),
        ],
        compiler_params=pltpu.CompilerParams(
            collective_id=0, has_side_effects=True, vmem_limit_bytes=66_000_000
        ),
    )(
        tokens.T,
        mod_scale,
        mod_shift,
        out_gate,
        w_query.T,
        w_key.T,
        w_value.T,
        w_out,
        mix_weight.reshape(NBR * TT, TT),
        log_decay,
        block_last,
        win_list.transpose(1, 2, 0).reshape(TILES * NBR, -1),
    )
    return out.T


def solution(mesh):
    placed = (
        P("tm", None),
        P(),
        P(),
        P(),
        P(None, "space"),
        P(None, "space"),
        P(None, "space"),
        P("space", None),
        P("tm", "space"),
        P(),
        P("tm"),
        P(),
    )
    return jax.shard_map(
        body, mesh=mesh, in_specs=placed, out_specs=P(("tm", "space"), None), check_vma=False
    )
```

```python
import jax
import jax.numpy as jnp
from jax import lax
from jax.experimental import pallas as pl
from jax.experimental.pallas import tpu as pltpu
from jax.sharding import PartitionSpec as P

HD = 112
NH = 5
GW = NH * HD
GP = 640
D = 2240
FR = 4
ROWS = 512
TILES = 32
TT = 16
NBR = 8
WIN = 2
PART = 288
EPS = 1e-06
RELS = (0, 2, 3, 1)
MESH = pl.DeviceIdType.MESH
BF = jnp.bfloat16
F32 = jnp.float32
NT = (((1,), (1,)), ((), ()))

X_GATHER = 0
FORWARD = 4
SIDE_PASS = 6
TWIN = 12
HALO = 15
SCAN = 17
SWAP = 25
MESSAGES = 31
HALF = 64


def kernel(
    tok_hbm, scale_ref, shift_ref, gate_ref, wq_hbm, wk_hbm, wv_hbm, wo_hbm, mix_ref,
    decay_ref, last_ref, list_ref, out_hbm,
    tok, resid, wqkv, wo_raw, wo, vbuf, kbuf, qbuf, win, mixb, acc, gains,
    relay, sloc, scur, entry, full_out, full_in, half_out, half_in, end_out, end_in,
    mixrep, rel, band, local_sem, send_sem, recv_sem,
):
    tm = lax.axis_index("tm")
    sp = lax.axis_index("space")
    z, y, core = tm // 8, (tm // 2) % 4, tm % 2

    def at(zz, yy, cc):
        return (zz * 8 + yy * 2 + cc, sp)

    def x_peer(step):
        return (tm, (sp + step) % 4)

    def z_peer(step):
        return at((z + step) % 4, y, core)

    def y_peer(step):
        return at(z, (y + step) % 4, core)

    twin = at(z, y, 1 - core)
    right = ((tm + 1) % 32, sp)
    left = ((tm + 31) % 32, sp)
    outer = ((tm + 31 + 2 * core) % 32, sp)

    def remote(number, src, dst, device):
        return pltpu.make_async_remote_copy(
            src_ref=src,
            dst_ref=dst,
            send_sem=send_sem.at[number],
            recv_sem=recv_sem.at[number],
            device_id=device,
            device_id_type=MESH,
        )

    def load(number, src, dst):
        return pltpu.make_async_copy(src, dst, local_sem.at[number])

    load_wo = load(0, wo_hbm, wo_raw.at[pl.ds(0, GW)])
    load_wv = load(1, wv_hbm, wqkv.at[0])
    load_wk = load(2, wk_hbm, wqkv.at[1])
    load_wq = load(3, wq_hbm, wqkv.at[2])
    own_rows = pl.ds(pl.multiple_of(sp * ROWS, ROWS), ROWS)
    load_resid = load(4, tok_hbm.at[:, own_rows], resid)

    def load_tok(f):
        rows = pl.ds(pl.multiple_of(f * ROWS, ROWS), ROWS)
        return load(5 + f, tok_hbm.at[:, rows], tok.at[f])

    load_wo.start()
    load_tok(0).start()
    load_wv.start()
    for f in range(1, FR):
        load_tok(f).start()
    load_wk.start()
    load_wq.start()
    load_resid.start()

    barrier = pltpu.get_barrier_semaphore()
    partners = [x_peer(i) for i in (1, 3)] + [y_peer(i) for i in (1, 2, 3)]
    partners += [z_peer(i) for i in (1, 2, 3)] + [twin, outer]
    for device in partners:
        pl.semaphore_signal(barrier, inc=1, device_id=device, device_id_type=MESH)

    def spots(rows, lanes, of_row, of_lane):
        r = lax.broadcasted_iota(jnp.int32, (rows, lanes), 0)
        l = lax.broadcasted_iota(jnp.int32, (rows, lanes), 1)
        return jnp.where(of_row(r) == of_lane(l), 1.0, 0.0).astype(BF)

    def exact(a, b, dims=(((1,), (0,)), ((), ()))):
        return lax.dot_general(a, b, dims, preferred_element_type=F32)

    for p in range(4):
        mixb[p * GP + GW : (p + 1) * GP, :] = jnp.zeros((GP - GW, ROWS), BF)

    wo_raw[GW:GP, :] = jnp.zeros((GP - GW, D), BF)
    wo[3, 1, D - 7 * PART : PART, 0:GP] = jnp.zeros((8 * PART - D, GP), BF)
    load_wo.wait()
    for low in range(0, D, 256):
        high = min(low + 256, D)
        eye = spots(high - low, high - low, lambda r: r, lambda l: l)
        turned = exact(eye, wo_raw[:, low:high], NT).astype(BF)
        for part in range(8):
            first, last = max(low, part * PART), min(high, (part + 1) * PART)
            if first < last:
                wo[part // 2, part % 2, first - part * PART : last - part * PART, 0:GP] = turned[
                    first - low : last - low
                ]

    pl.semaphore_wait(barrier, len(partners))

    def chunk(p, i):
        return wo.at[i, core, :, pl.ds(p * GP, GP)]

    onward = x_peer(1 + 2 * core)

    def place(p):
        if p == 2:
            return z, z_peer
        if p == 3:
            return y, y_peer
        return z + core * (y - z), lambda step: at(
            (z + (1 - core) * step) % 4, (y + core * step) % 4, core
        )

    def x_gather(p, second):
        i = (place(p)[0] + second) % 4
        number = X_GATHER + (p - 2) * 2 + second
        return remote(number, chunk(0, i), chunk(p, i), x_peer(4 - RELS[p]))

    def x_forward(second):
        i = (place(1)[0] + second) % 4
        cols = pl.ds(pl.multiple_of((2 + core) * GP, 128), GP)
        return remote(FORWARD + second, wo.at[i, core, :, cols], chunk(1, i), onward)

    def side_pass(p, second):
        i, peer = place(p)
        ref = chunk(p, (i + second) % 4)
        return remote(SIDE_PASS + (p - 1) * 2 + second, ref, ref, peer(3 if second else 1))

    def x_arrived(second):
        for p in (2, 3):
            x_gather(p, second).wait_recv()
            side_pass(p, second).start()
        x_forward(second).start()

    def to_twin(p):
        ref = wo.at[:, core, :, pl.ds(p * GP, GP)]
        return remote(TWIN + p - 1, ref, ref, twin)

    for second in (0, 1):
        for p in (2, 3):
            x_gather(p, second).start()

    parts = []
    for vector in (1.0 + scale_ref[...], shift_ref[...], gate_ref[...]):
        rest = vector.reshape(1, D)
        for _ in range(3):
            part = rest.astype(BF)
            parts.append(part)
            rest = rest - part.astype(F32)
    parts = jnp.concatenate(parts + [jnp.zeros((7, D), BF)], axis=0)
    gains[...] = exact(
        parts, spots(16, 384, lambda r: r // 3, lambda l: l // 128), (((0,), (0,)), ((), ()))
    )

    def norm(f):
        def squares(i, total):
            x = tok[f, pl.ds(pl.multiple_of(i * 112, 112), 112), :].astype(F32)
            return total + jnp.sum((x * x).reshape(112 // 8, 8, ROWS), axis=0)

        total = lax.fori_loop(0, D // 112, squares, jnp.zeros((8, ROWS), F32))
        inverse = lax.rsqrt(jnp.sum(total, axis=0, keepdims=True) * (1.0 / D) + EPS)

        def scale(i, _):
            r = pl.ds(pl.multiple_of(i * 64, 64), 64)
            gain = jnp.concatenate([gains[r, 0:128]] * (ROWS // 128), axis=1)
            shift = jnp.concatenate([gains[r, 128:256]] * (ROWS // 128), axis=1)
            x = tok[f, r, :].astype(F32)
            tok[f, r, :] = (x * inverse * gain + shift).astype(BF)
            return 0

        lax.fori_loop(0, D // 64, scale, 0)

    def halo_left():
        return remote(HALO, vbuf.at[pl.ds(2, 2)], vbuf.at[pl.ds(6, 2)], left)

    def halo_right():
        return remote(HALO + 1, vbuf.at[pl.ds(4, 2)], vbuf.at[pl.ds(0, 2)], right)

    def decay(f, h):
        return jnp.exp(jnp.full((1, HD), decay_ref[f, h], F32))

    def project(weight, f, dst):
        dst[...] = exact(wqkv[weight], tok[f]).astype(BF)

    @pl.when(tm == 0)
    def _():
        vbuf[0:2] = jnp.zeros((2, GW, ROWS), BF)

    @pl.when(tm == 31)
    def _():
        vbuf[6:8] = jnp.zeros((2, GW, ROWS), BF)

    load_wv.wait()

    def value(f, _):
        load_tok(f).wait()
        norm(f)
        project(0, f, vbuf.at[2 + f])

        @pl.when(f == 1)
        def _():
            @pl.when(tm > 0)
            def _():
                halo_left().start()

        @pl.when(f == 2)
        def _():
            x_arrived(0)

        @pl.when(f == 3)
        def _():
            @pl.when(tm < 31)
            def _():
                halo_right().start()

        return 0

    lax.fori_loop(0, FR, value, 0)

    load_wk.wait()
    scur[...] = jnp.zeros_like(scur)

    def key(f, _):
        project(1, f, kbuf)
        for h in range(NH):
            rows = slice(h * HD, (h + 1) * HD)
            fresh = exact(vbuf[2 + f, rows, :], kbuf[rows, :], NT)
            state = decay(f, h) * scur[h, 0:HD, :] + fresh
            scur[h, 0:HD, :] = state
            sloc[f, h] = state

        @pl.when(f == 2)
        def _():
            x_arrived(1)

        return 0

    lax.fori_loop(0, FR, key, 0)

    row_id = lax.broadcasted_iota(jnp.int32, (TT, HD), 0)
    half_rows = pl.ds(pl.multiple_of(core * HALF, HALF), HALF)
    other_rows = pl.ds(pl.multiple_of((1 - core) * HALF, HALF), HALF)

    def put_log(ref, log):
        high = log.astype(BF).astype(F32)
        low = log - high
        ref[...] = jnp.where(row_id == 0, high, jnp.where(row_id == 1, low, 0.0)).astype(BF)

    def get_log(ref):
        return jnp.sum(ref[...].astype(F32), axis=0, keepdims=True)

    def flag(condition):
        return jnp.where(condition, 1.0, 0.0).astype(F32)

    def join(early, late):
        return early[0] + late[0], jnp.exp(late[0]) * early[1] + late[1]

    def choose(on, pair, other):
        return tuple(on * a + (1.0 - on) * b for a, b in zip(pair, other))

    def masked(on, pair):
        return tuple(on * a for a in pair)

    def own_log(h):
        log = jnp.full((1, HD), decay_ref[0, h], F32)
        for f in range(1, FR):
            log = log + jnp.full((1, HD), decay_ref[f, h], F32)
        return log

    first_core = flag(core == 0)

    def chip_pair(h):
        own = own_log(h), scur[h, half_rows, :]
        other = get_log(full_in.at[h, 128:144]), full_in[h, half_rows, :].astype(F32)
        return join(choose(first_core, own, other), choose(first_core, other, own))

    def put(slot, pairs):
        logs = jnp.zeros((TT, HD), F32)
        for h, (log, state) in enumerate(pairs):
            half_out[slot, h * HALF : (h + 1) * HALF, :] = state.astype(BF)
            high = log.astype(BF).astype(F32)
            logs = jnp.where(row_id == 2 * h, high, logs)
            logs = jnp.where(row_id == 2 * h + 1, log - high, logs)
        half_out[slot, NH * HALF :, :] = logs.astype(BF)

    def get(slot, h):
        logs = half_in[slot, NH * HALF :, :].astype(F32)
        log = jnp.sum(jnp.where(row_id // 2 == h, logs, 0.0), axis=0, keepdims=True)
        return log, half_in[slot, h * HALF : (h + 1) * HALF, :].astype(F32)

    def scan_core():
        return remote(SCAN, full_out, full_in, twin)

    def scan_y(step):
        return remote(SCAN + step, half_out.at[0], half_in.at[step - 1], y_peer(step))

    def scan_z(step):
        return remote(SCAN + 3 + step, half_out.at[1], half_in.at[2 + step], z_peer(step))

    def scan_end():
        return remote(SCAN + 7, end_out, end_in, twin)

    def prefix(place, slot, h):
        total = None
        for step in (3, 2, 1):
            pair = masked(flag(place >= step), get(slot + step, h))
            total = pair if total is None else join(total, pair)
        return total

    for h in range(NH):
        full_out[h, 0:128, :] = scur[h].astype(BF)
        put_log(full_out.at[h, 128:144], own_log(h))
    scan_core().start()

    def frame_of(p):
        return (sp + 4 - RELS[p]) % 4

    load_wq.wait()

    def query(p):
        project(2, frame_of(p), qbuf.at[frame_of(p)])

    query(1)

    scan_core().wait_recv()
    put(0, [chip_pair(h) for h in range(NH)])
    for step in (1, 2, 3):
        scan_y(step).start()

    query(2)
    mixed_t = exact(spots(TT, TT, lambda r: r, lambda l: l), mix_ref[...], NT).astype(BF)
    mine = exact(
        spots(8, 128, lambda r: r + FR * tm, lambda l: l), list_ref[...].astype(BF), NT
    )
    mine = (mine - (FR * tm - WIN).astype(F32)).astype(BF)
    for n in range(NBR):
        mixrep[n] = exact(
            mixed_t, spots(128, 128, lambda r: r, lambda l: l % TT + n * TT)
        )
        listed = exact(
            mine, spots(TILES * NBR, ROWS, lambda r: r, lambda l: l // TT * NBR + n)
        )
        for f in range(FR):
            rel[f, n : n + 1, :] = listed[f : f + 1]

    query(3)

    for step in (1, 2, 3):
        scan_y(step).wait_recv()
    totals = []
    for h in range(NH):
        total = join(prefix(y, -1, h), chip_pair(h))
        for step in (3, 2, 1):
            total = join(total, masked(flag(y < step), get(step - 1, h)))
        totals.append(total)
    put(1, totals)
    for step in (1, 2, 3):
        scan_z(step).start()

    @pl.when(tm < 31)
    def _():
        halo_left().wait_recv()

    @pl.when(tm > 0)
    def _():
        halo_right().wait_recv()

    tile_of_lane = lax.broadcasted_iota(jnp.int32, (TT, 128), 1) // TT

    def window(p):
        f = frame_of(p)

        def tiles(j, _):
            cols = pl.ds(pl.multiple_of(j * 128, 128), 128)
            for g in range(2 * WIN + 1):
                block = jnp.zeros((TT, 128), F32)
                for n in range(NBR):
                    listed = rel[f, n : n + 1, cols]
                    block = block + jnp.where(listed == (f + g).astype(F32), mixrep[n], 0.0)
                for t in range(8):
                    low = g * 128 + t * TT
                    band[low : low + TT, :] = jnp.where(tile_of_lane == t, block, 0.0).astype(BF)
            source = jnp.concatenate([vbuf[f + g, :, cols] for g in range(2 * WIN + 1)], axis=1)
            win[f, :, cols] = exact(source, band[...]).astype(BF)
            return 0

        lax.fori_loop(0, ROWS // 128, tiles, 0)

    window(1)
    window(2)

    for step in (1, 2, 3):
        scan_z(step).wait_recv()
    for h in range(NH):
        half = join(prefix(z, 2, h), prefix(y, -1, h))[1]
        entry[h, half_rows, :] = half
        end_out[h] = half.astype(BF)
    scan_end().start()

    for second in (0, 1):
        x_forward(second).wait_recv()
        side_pass(1, second).start()
    for p in (2, 3):
        side_pass(p, 0).wait_recv()
        side_pass(p, 1).wait_recv()
        to_twin(p).start()

    window(3)

    scan_end().wait_recv()
    for h in range(NH):
        entry[h, other_rows, :] = end_in[h].astype(F32)
        before = get_log(full_in.at[h, 128:144]), full_in[h, 0:HD, :].astype(F32)
        before = masked(1.0 - first_core, before)
        entering = jnp.exp(before[0]) * entry[h, 0:HD, :] + before[1]
        for f in range(FR):
            entering = decay(f, h) * entering
            sloc[f, h] = sloc[f, h] + entering

    def swap(p):
        return remote(
            SWAP + p - 2,
            qbuf.at[frame_of(p)],
            mixb.at[pl.ds(p * GP, GW)],
            x_peer(4 - RELS[p]),
        )

    def far(leg, half):
        cols = pl.ds(half * 256, 256)
        refs = qbuf.at[frame_of(1), :, cols], relay.at[:, cols], mixb.at[pl.ds(GP, GW), cols]
        return remote(SWAP + 2 + leg * 2 + half, refs[leg], refs[leg + 1], onward)

    def attend(p, low=0, high=ROWS):
        f = frame_of(p)
        cols = slice(low, high)
        for h in range(NH):
            rows = slice(h * HD, (h + 1) * HD)
            state = jnp.zeros((HD, HD), F32)
            for g in range(FR):
                state = state + flag(last_ref[f] == FR * tm + g) * sloc[g, h]
            linear = exact(state.astype(BF), qbuf[f, rows, cols])
            inverse = lax.rsqrt(
                jnp.sum(linear * linear, axis=0, keepdims=True) * (1.0 / HD) + EPS
            )
            both = (linear * inverse + win[f, rows, cols].astype(F32)).astype(BF)
            if p == 0:
                mixb[rows, cols] = both
            else:
                qbuf[f, rows, cols] = both

    for half in range(2):
        attend(1, half * 256, (half + 1) * 256)
        far(0, half).start()
    for p in (2, 3):
        attend(p)
        swap(p).start()
    query(0)
    far(0, 0).wait_recv()
    far(1, 0).start()
    window(0)
    attend(0)
    far(0, 1).wait_recv()
    far(1, 1).start()
    side_pass(1, 0).wait_recv()
    side_pass(1, 1).wait_recv()
    to_twin(1).start()

    load_resid.wait()

    def weights(i, p, count):
        return wo[i, :, :, p * GP : (p + count) * GP].reshape(2 * PART, count * GP)

    for i in range(4):
        low, high = i * 2 * PART, min((i + 1) * 2 * PART, D)
        acc[low:high, :] = exact(weights(i, 0, 1)[: high - low], mixb[0:GP, :])

    for p in (2, 3):
        to_twin(p).wait_recv()
        swap(p).wait_recv()
    for i in range(4):
        low, high = i * 2 * PART, min((i + 1) * 2 * PART, D)
        acc[low:high, :] += exact(weights(i, 2, 2)[: high - low], mixb[2 * GP : 4 * GP, :])

    def store(i, half):
        rows = pl.ds(i * 2 * PART, min(2 * PART, D - i * 2 * PART))
        cols = pl.ds(half * 256, 256)
        return load(9 + i + 4 * half, resid.at[rows, cols], out_hbm.at[rows, cols])

    to_twin(1).wait_recv()
    for half in range(2):
        far(1, half).wait_recv()
        now = slice(half * 256, (half + 1) * 256)
        for i in range(4):
            low, high = i * 2 * PART, min((i + 1) * 2 * PART, D)
            total = acc[low:high, now] + exact(
                weights(i, 1, 1)[: high - low], mixb[GP : 2 * GP, now]
            )
            for c in range(2):
                cols = slice(half * 256 + c * 128, half * 256 + (c + 1) * 128)
                resid[low:high, cols] = (
                    resid[low:high, cols].astype(F32)
                    + gains[low:high, 256:384] * total[:, c * 128 : (c + 1) * 128]
                ).astype(BF)
            store(i, half).start()

    for p in (1, 2, 3):
        to_twin(p).wait_send()
        if p > 1:
            swap(p).wait_send()
        scan_y(p).wait_send()
        scan_z(p).wait_send()
    for second in (0, 1):
        for p in (1, 2, 3):
            side_pass(p, second).wait_send()
            if p > 1:
                x_gather(p, second).wait_send()
        x_forward(second).wait_send()
    for half in range(2):
        for leg in range(2):
            far(leg, half).wait_send()
    scan_core().wait_send()
    scan_end().wait_send()

    @pl.when(tm > 0)
    def _():
        halo_left().wait_send()

    @pl.when(tm < 31)
    def _():
        halo_right().wait_send()

    for half in range(2):
        for i in range(4):
            store(i, half).wait()


def body(
    tokens, mod_scale, mod_shift, out_gate, w_query, w_key, w_value, w_out,
    log_decay, mix_weight, block_last, win_list,
):
    anywhere = pl.BlockSpec(memory_space=pl.ANY)
    vmem = pl.BlockSpec(memory_space=pltpu.VMEM)
    smem = pl.BlockSpec(memory_space=pltpu.SMEM)
    out = pl.pallas_call(
        kernel,
        out_shape=jax.ShapeDtypeStruct((D, ROWS), BF),
        in_specs=[anywhere, vmem, vmem, vmem] + [anywhere] * 4 + [vmem, smem, smem, vmem],
        out_specs=anywhere,
        scratch_shapes=[
            pltpu.VMEM((FR, D, ROWS), BF),
            pltpu.VMEM((D, ROWS), BF),
            pltpu.VMEM((3, GW, D), BF),
            pltpu.VMEM((GP, D), BF),
            pltpu.VMEM((4, 2, PART, 4 * GP), BF),
            pltpu.VMEM((2 * FR, GW, ROWS), BF),
            pltpu.VMEM((GW, ROWS), BF),
            pltpu.VMEM((FR, GW, ROWS), BF),
            pltpu.VMEM((FR, GW, ROWS), BF),
            pltpu.VMEM((4 * GP, ROWS), BF),
            pltpu.VMEM((D, ROWS), F32),
            pltpu.VMEM((D, 384), F32),
            pltpu.VMEM((GW, ROWS), BF),
            pltpu.VMEM((FR, NH, HD, HD), F32),
            pltpu.VMEM((NH, 128, HD), F32),
            pltpu.VMEM((NH, 128, HD), F32),
            pltpu.VMEM((NH, 144, HD), BF),
            pltpu.VMEM((NH, 144, HD), BF),
            pltpu.VMEM((2, NH * HALF + TT, HD), BF),
            pltpu.VMEM((6, NH * HALF + TT, HD), BF),
            pltpu.VMEM((NH, HALF, HD), BF),
            pltpu.VMEM((NH, HALF, HD), BF),
            pltpu.VMEM((NBR, TT, 128), F32),
            pltpu.VMEM((FR, NBR, ROWS), F32),
            pltpu.VMEM(((2 * WIN + 1) * 128, 128), BF),
            pltpu.SemaphoreType.DMA((17,)),
            pltpu.SemaphoreType.DMA((MESSAGES,)),
            pltpu.SemaphoreType.DMA((MESSAGES,)),
        ],
        compiler_params=pltpu.CompilerParams(
            collective_id=0, has_side_effects=True, vmem_limit_bytes=66_000_000
        ),
    )(
        tokens.T,
        mod_scale,
        mod_shift,
        out_gate,
        w_query.T,
        w_key.T,
        w_value.T,
        w_out,
        mix_weight.reshape(NBR * TT, TT),
        log_decay,
        block_last,
        win_list.transpose(1, 2, 0).reshape(TILES * NBR, -1),
    )
    return out.T


def solution(mesh):
    placed = (
        P("tm", None),
        P(),
        P(),
        P(),
        P(None, "space"),
        P(None, "space"),
        P(None, "space"),
        P("space", None),
        P("tm", "space"),
        P(),
        P("tm"),
        P(),
    )
    return jax.shard_map(
        body, mesh=mesh, in_specs=placed, out_specs=P(("tm", "space"), None), check_vma=False
    )
```
